256 devices in a mesh: row: 8 (over x, z_lo), col: 32 (over z_hi, y, core).
Axes of the slice: x: 4, y: 4, z: 8 (z_hi: 4, z_lo: 2; z = z_hi * 2 + z_lo), core: 2. Of those that a mesh axis runs over, the one named last changes fastest.
Arguments:
- activations: bfloat16 [4096, 2560], P('col', 'row'), may hold values from -6 to 6
- cotangent: bfloat16 [4096, 6912], P('row', 'col'), may hold values from -6 to 6
- small_weight: bfloat16 [2048, 5504], P('row', 'col'), may hold values from -0.125 to 0.125
- grow_rows: bfloat16 [2560, 2048], P('row', 'col'), may hold values from -0.125 to 0.125
- grow_cols: bfloat16 [6912, 5504], P('col', 'row'), may hold values from -0.15625 to 0.15625
Outputs:
- grad_rows: bfloat16 [2560, 2048], P('row', 'col')
- grad_cols: bfloat16 [6912, 5504], P('col', 'row')
- grad_small: bfloat16 [2048, 5504], P('row', 'col')
The draws below stay inside these ranges and needn't reach their ends.
All inputs are finite; a program needn't handle non-finite values.
Results may differ from the reference program's by a relative error of at most 0.015.
Values may be sent and summed in bfloat16 or wider, within the bound.
A program may use at most 64 MiB of HBM per device.

```python
import jax
import jax.numpy as jnp

D0 = 2048
D1 = 2560
F0 = 5504
F1 = 6912
TOKENS = 4096


def with_spikes(array, rng, source, target, blocks, factor):
    owner, partner = [(jnp.arange(array.shape[position]) // (array.shape[position] // blocks)).reshape([-1 if axis == position else 1 for axis in range(array.ndim)]) for position in (source, target)]
    chosen = jax.random.permutation(rng, blocks)[partner]
    strong = (owner == chosen) | (owner == (partner + blocks // 2) % blocks)
    return jnp.where(strong, factor * array, array)


def block_scale(own_key, shape, shards, smallest, high):
    def one(dim, shards_of):
        heights = jax.random.uniform(jax.random.fold_in(jax.random.fold_in(own_key, 6), dim), (shards_of,), jnp.float32, smallest / len(shards), high / len(shards))
        return jnp.repeat(jnp.exp(heights), shape[dim] // shards_of).reshape((-1,) + (1,) * (len(shape) - dim - 1))

    gain = one(*shards[0])
    for cut in shards[1:]:
        gain = gain * one(*cut)
    return gain


def centred(own_key, shape, scale, bound, split=(), held_as=jnp.bfloat16):
    factor_of = block_scale(own_key, shape, split, -0.22, 0.18) if split else 1.0
    entries = jax.random.normal(own_key, shape, jnp.float32) * scale * factor_of
    return jnp.minimum(jnp.maximum(entries, -bound), bound).astype(held_as)


def bell_draw_with(own_key, shape, deviation, most, shards, heavy, dtype=jnp.bfloat16):
    values = deviation * jax.random.normal(own_key, shape, jnp.float32)
    if shards:
        values = values * block_scale(own_key, shape, shards, -0.22, 0.18)
    return jnp.clip(with_spikes(values, jax.random.fold_in(own_key, 3), *heavy), -most, most).astype(dtype)


def setup_inputs(seed: int = 0) -> dict:
    streams_of = jax.random.split(jax.random.key(seed), 6)
    return {
        "activations": centred(streams_of[0], (TOKENS, D1), 1.0, 6.0, ((0, 32), (1, 8))),
        "cotangent": centred(streams_of[1], (TOKENS, F1), 1.0, 6.0, ((0, 8), (1, 32))),
        "small_weight": centred(streams_of[2], (D0, F0), D0 ** -0.5, 0.125, ((0, 8), (1, 32))),
        "grow_rows": centred(streams_of[3], (D1, D0), D0 ** -0.5, 0.125, ((0, 8), (1, 32))),
        "grow_cols": bell_draw_with(streams_of[4], (F1, F0), F0 ** -0.5, 0.15625, ((0, 32), (1, 8)), (0, 1, 32, 2.75)),
    }


def reference(activations, cotangent, small_weight, grow_rows, grow_cols):
    chain = jnp.dot(small_weight, grow_cols.T, preferred_element_type=jnp.float32).astype(jnp.bfloat16)
    grown = jnp.dot(grow_rows, chain, preferred_element_type=jnp.float32).astype(jnp.bfloat16)
    hidden = jnp.dot(activations, grown, preferred_element_type=jnp.float32)
    squash = jax.nn.sigmoid(hidden)
    delta = (cotangent.astype(jnp.float32) * squash * (1.0 + hidden * (1.0 - squash))).astype(jnp.bfloat16)
    norm_scale = jnp.float32(activations.shape[0]) ** -0.5
    grad_grown = (jnp.dot(activations.T, delta, preferred_element_type=jnp.float32) * norm_scale).astype(jnp.bfloat16)
    grad_rows = jnp.dot(grad_grown, chain.T, preferred_element_type=jnp.float32).astype(jnp.bfloat16)
    back_panel = jnp.dot(grow_rows.T, grad_grown, preferred_element_type=jnp.float32).astype(jnp.bfloat16)
    grad_cols = jnp.dot(back_panel.T, small_weight, preferred_element_type=jnp.float32).astype(jnp.bfloat16)
    grad_small = jnp.dot(back_panel, grow_cols, preferred_element_type=jnp.float32).astype(jnp.bfloat16)
    return grad_rows, grad_cols, grad_small
```

```python
import functools

import jax
import jax.numpy as jnp
from jax import lax
from jax.experimental import pallas as pl
from jax.experimental.pallas import tpu as pltpu
from jax.sharding import PartitionSpec as P

MESH = pl.DeviceIdType.MESH
F32 = jnp.float32
BF16 = jnp.bfloat16
HW = 176
HP = 128
FP = 224
HA = 160
NSEM = 128
KT = (0, 2, 1, 3)


def nn(a, b):
    return jnp.dot(a, b, preferred_element_type=F32)


def nt(a, b):
    return lax.dot_general(a, b, (((1,), (1,)), ((), ())), preferred_element_type=F32)


def lanes(start, size):
    return pl.ds(pl.multiple_of(start, 128), size)


def rows(start, size):
    return pl.ds(pl.multiple_of(start, 16), size)


def kernel(
    scale,
    act, cot, w, a, b,
    gr_out, gc_out, gs_out,
    wpad, wsend, wbuf, aown, ax, abuf, bp, bpt, actp, att,
    ps, prcv, pblk, pbuf,
    cs, crcv, ct, delta, dt,
    bs, brcv, bt,
    qs, qc, qo, qh, qry, qzf, qzs, qrz, qfin, qt,
    gs, gc, go, gh, gry, gzf, gzs, grz, gfin, gst,
    hs, hc, ho, hh, hry, hzf, hzs, hrz, hfin, hp,
    ssem, rsem, lsem,
):
    r = lax.axis_index("row")
    c = lax.axis_index("col")
    x, zlo = r // 2, r % 2
    zhi, y, core = c // 8, (c // 2) % 4, c % 2
    yh, yl = y // 2, y % 2
    kt = 2 * core + yl
    far = 1 - core

    def row_peer(d):
        return ((r + d) % 8, c)

    def y_peer(d):
        return (r, zhi * 8 + ((y + d) % 4) * 2 + core)

    def z_peer(d):
        return (r, ((zhi + d) % 4) * 8 + y * 2 + core)

    core_peer = (r, c + 1 - 2 * core)
    t_peer = (zhi * 2 + yh, x * 8 + zlo * 4 + yl * 2 + core)
    stays = jnp.logical_and(x == zhi, zlo == yh)
    moves = jnp.logical_not(stays)

    used = [0]
    sent = []

    def push(src, dst, device):
        i = used[0]
        used[0] += 1
        copy = pltpu.make_async_remote_copy(
            src_ref=src, dst_ref=dst, send_sem=ssem.at[i], recv_sem=rsem.at[i],
            device_id=device, device_id_type=MESH,
        )
        copy.start()
        sent.append(copy)
        return copy

    swaps = []

    def swap(src, dst):
        i = used[0]
        used[0] += 1
        remote = pltpu.make_async_remote_copy(
            src_ref=src, dst_ref=dst, send_sem=ssem.at[i], recv_sem=rsem.at[i],
            device_id=t_peer, device_id_type=MESH,
        )
        local = pltpu.make_async_copy(src, dst, lsem.at[len(swaps)])

        @pl.when(moves)
        def _():
            remote.start()

        @pl.when(stays)
        def _():
            local.start()

        swaps.append(remote)

        def wait():
            @pl.when(moves)
            def _():
                remote.wait_recv()

            @pl.when(stays)
            def _():
                local.wait()

        return wait

    barrier = pltpu.get_barrier_semaphore()
    for d in range(1, 8):
        pl.semaphore_signal(barrier, inc=1, device_id=row_peer(d), device_id_type=MESH)
    for d in range(1, 4):
        pl.semaphore_signal(barrier, inc=1, device_id=y_peer(d), device_id_type=MESH)
        pl.semaphore_signal(barrier, inc=1, device_id=z_peer(d), device_id_type=MESH)
    pl.semaphore_signal(barrier, inc=1, device_id=core_peer, device_id_type=MESH)

    @pl.when(moves)
    def _():
        pl.semaphore_signal(barrier, inc=1, device_id=t_peer, device_id_type=MESH)

    aown[:, 0:64] = a[...]
    aown[:, 64:128] = a[...]
    wpad[...] = jnp.zeros_like(wpad)
    wpad[:, 0:172] = w[...]
    wsend[...] = wpad[...].T[0:HW]

    @pl.when(moves)
    def _():
        pl.semaphore_wait(barrier, 15)

    @pl.when(stays)
    def _():
        pl.semaphore_wait(barrier, 14)

    slot = lanes(1024 * yh + 256 * zhi, 256)
    band = lanes(1024 * yh, 1024)
    t_slot = lanes(1024 * zlo + 256 * x, 256)
    wrow = rows(HW * kt, HW)
    prow = rows(HP * kt, HP)

    a_pair = push(aown.at[rows(HA * far, HA), :], ax, core_peer)
    w_swap = swap(wsend, wbuf.at[wrow, t_slot])

    a_pair.wait_recv()
    lane = lax.broadcasted_iota(jnp.int32, (HA, 128), 1)
    arow = rows(HA * core, HA)
    abuf[y, arow, lanes(128 * zhi, 128)] = jnp.where(lane // 64 == core, aown[arow, :], ax[...])

    def gather_z(block):
        return [push(block, block, z_peer(d)) for d in (1, 2, 3)]

    def gather_y(block):
        return [push(block, block, y_peer(d)) for d in (1, 2, 3)]

    def wait_all(copies):
        for copy in copies:
            copy.wait_recv()

    a_z = gather_z(abuf.at[y, arow, lanes(128 * zhi, 128)])
    w_swap()
    w_z = gather_z(wbuf.at[wrow, slot])

    wait_all(a_z)
    a_y = gather_y(abuf.at[y, arow, :])
    a_core = [push(abuf.at[y, arow, :], abuf.at[y, arow, :], core_peer)]
    wait_all(w_z)
    w_y = gather_y(wbuf.at[wrow, band])
    w_core = [push(wbuf.at[wrow, band], wbuf.at[wrow, band], core_peer)]

    bp[...] = jnp.zeros_like(bp)
    for k in range(4):
        bp[0:216, HW * KT[k]:HW * KT[k] + 172] = b[:, 172 * k:172 * k + 172]
    bpt[...] = bp[...].T

    for d in (1, 2, 3):
        a_y[d - 1].wait_recv()
        block = abuf.at[(y + 4 - d) % 4, arow, :]
        a_core.append(push(block, block, core_peer))
    wait_all(a_core)

    for q in range(4):
        part = nn(act[...], abuf[q]).astype(BF16)
        for z in range(4):
            ps[2 * z + q // 2, :, 128 * (q % 2):128 * (q % 2) + 128] = part[:, 128 * z:128 * z + 128]
    p_rs = [push(ps.at[(r + d) % 8], prcv.at[d - 1], row_peer(d)) for d in range(1, 8)]

    for d in (1, 2, 3):
        w_y[d - 1].wait_recv()
        other = (y + 4 - d) % 4
        block = wbuf.at[rows(HW * (2 * core + other % 2), HW), lanes(1024 * (other // 2), 1024)]
        w_core.append(push(block, block, core_peer))

    wait_all(p_rs)
    total = ps[r].astype(F32)
    for d in range(7):
        total = total + prcv[d].astype(F32)
    pblk[...] = total.astype(BF16)
    p_swap = swap(pblk, pbuf.at[prow, t_slot])

    wait_all(w_core)
    c_rs = []
    for d in range(1, 8):
        peer = (r + d) % 8
        cs[d - 1] = nn(bp[0:FP, 0:4 * HW], wbuf[:, lanes(1024 * (peer % 2) + 256 * (peer // 2), 256)]).astype(BF16)
        c_rs.append(push(cs.at[d - 1], crcv.at[d - 1], row_peer(d)))
    own = lanes(1024 * zlo + 256 * x, 256)
    total = nn(bp[0:FP, 0:4 * HW], wbuf[:, own])

    p_swap()
    p_z = gather_z(pbuf.at[prow, slot])

    for d in range(7):
        c_rs[d].wait_recv()
        total = total + crcv[d].astype(F32)
    ct[:, own] = total.astype(BF16)
    c_ag = [push(ct.at[:, own], ct.at[:, own], row_peer(d)) for d in range(1, 8)]

    wait_all(p_z)
    p_y = gather_y(pbuf.at[prow, band])
    p_core = [push(pbuf.at[prow, band], pbuf.at[prow, band], core_peer)]
    delta[...] = jnp.zeros_like(delta)
    actp[...] = jnp.zeros_like(actp)
    actp[:, 0:320] = act[...]
    att[...] = actp[...].T
    for d in (1, 2, 3):
        p_y[d - 1].wait_recv()
        other = (y + 4 - d) % 4
        block = pbuf.at[rows(HP * (2 * core + other % 2), HP), lanes(1024 * (other // 2), 1024)]
        p_core.append(push(block, block, core_peer))
    wait_all(p_core)
    wait_all(c_ag)

    for k in range(4):
        t = KT[k]
        hidden = nt(pbuf[HP * t:HP * t + HP, :], ct[...])[:, 0:216]
        s = 1.0 / (1.0 + jnp.exp(-hidden))
        grad = cot[HP * k:HP * k + HP, :].astype(F32) * s * (1.0 + hidden * (1.0 - s))
        delta[HP * t:HP * t + HP, 0:216] = grad.astype(BF16)
    dt[...] = delta[...].T

    b_rs = []
    for d in range(1, 8):
        peer = (r + d) % 8
        bs[d - 1] = nn(dt[0:FP, :], pbuf[:, lanes(1024 * (peer % 2) + 256 * (peer // 2), 256)]).astype(BF16)
        b_rs.append(push(bs.at[d - 1], brcv.at[d - 1], row_peer(d)))

    def tiles(body):
        lax.fori_loop(0, 8, lambda i, _: (body(lanes(256 * i, 256)), 0)[1], 0)

    def q_far(at):
        qs[:, at] = nn(delta[rows(2 * HP * far, 2 * HP), 0:FP], ct[:, at]).astype(BF16)

    def q_own(at):
        qo[:, at] = nn(delta[rows(2 * HP * core, 2 * HP), 0:FP], ct[:, at])

    tiles(q_far)
    q_core = push(qs, qc, core_peer)
    tiles(q_own)
    total = nn(dt[0:FP, :], pbuf[:, own])
    q_core.wait_recv()

    def q_sum(at):
        value = qo[:, at] + qc[:, at].astype(F32)
        qo[:, at] = value
        qh[:, at] = value.astype(BF16)

    tiles(q_sum)

    def scatter_y(half, height, into):
        copies = []
        for d in (1, 2, 3):
            other = (y + d) % 4
            copies.append(push(
                half.at[rows(height * (other % 2), height), lanes(1024 * (other // 2), 1024)],
                into.at[d - 1], y_peer(d)))
        return copies

    def scatter_z(part, width, into):
        return [
            push(part.at[:, lanes(width * ((zhi + d) % 4), width)], into.at[d - 1], z_peer(d))
            for d in (1, 2, 3)
        ]

    q_y = scatter_y(qh, HP, qry)

    for d in range(7):
        b_rs[d].wait_recv()
        total = total + brcv[d].astype(F32)
    bt[:, own] = (total * scale).astype(BF16)
    b_ag = [push(bt.at[:, own], bt.at[:, own], row_peer(d)) for d in range(1, 8)]

    def sum_y(copies, full, height, received, wide, narrow):
        wait_all(copies)
        for z in range(4):
            at = slice(256 * z, 256 * z + 256)
            value = full[rows(height * yl, height), lanes(1024 * yh + 256 * z, 256)]
            for d in range(3):
                value = value + received[d, :, at].astype(F32)
            wide[:, at] = value
            narrow[:, at] = value.astype(BF16)

    def sum_z(copies, wide, width, received):
        wait_all(copies)
        value = wide[:, lanes(width * zhi, width)]
        for d in range(3):
            value = value + received[d].astype(F32)
        return value

    sum_y(q_y, qo, HP, qry, qzf, qzs)
    q_z = scatter_z(qzs, 256, qrz)
    qfin[...] = (sum_z(q_z, qzf, 256, qrz) * scale).astype(BF16)
    q_swap = swap(qfin, qt.at[:, slot])

    wait_all(b_ag)

    def g_far(at):
        gs[:, at] = nn(bpt[rows(2 * HW * far, 2 * HW), 0:FP], bt[:, at]).astype(BF16)

    def g_own(at):
        go[:, at] = nn(bpt[rows(2 * HW * core, 2 * HW), 0:FP], bt[:, at])

    tiles(g_far)
    g_core = push(gs, gc, core_peer)
    q_swap()
    q_ag = [push(qt.at[:, own], qt.at[:, own], row_peer(d)) for d in range(1, 8)]
    tiles(g_own)
    g_core.wait_recv()

    def g_sum(at):
        value = go[:, at] + gc[:, at].astype(F32)
        go[:, at] = value
        gh[:, at] = value.astype(BF16)

    tiles(g_sum)
    g_y = scatter_y(gh, HW, gry)

    for t in range(4):
        gc_out[:, HW * t:HW * t + HW] = nt(bt[...], wbuf[HW * t:HW * t + HW, :]).astype(BF16)

    wait_all(q_ag)
    for q in range(8):
        part = nn(att[rows(HA * far, HA), :], qt[:, 256 * q:256 * q + 256]).astype(BF16)
        for v in range(2):
            hs[2 * (q // 4) + v, :, 128 * (q % 4):128 * (q % 4) + 128] = part[:, 128 * v:128 * v + 128]
    h_core = push(hs, hc, core_peer)
    for q in range(8):
        part = nn(att[arow, :], qt[:, 256 * q:256 * q + 256])
        for v in range(2):
            ho[2 * (q // 4) + v, :, 128 * (q % 4):128 * (q % 4) + 128] = part[:, 128 * v:128 * v + 128]
    h_core.wait_recv()
    for q in range(4):
        value = ho[q] + hc[q].astype(F32)
        ho[q] = value
        hh[q] = value.astype(BF16)
    h_y = [push(hh.at[(y + d) % 4], hry.at[d - 1], y_peer(d)) for d in (1, 2, 3)]

    sum_y(g_y, go, HW, gry, gzf, gzs)
    g_z = scatter_z(gzs, 256, grz)

    wait_all(h_y)
    value = ho[y]
    for d in range(3):
        value = value + hry[d].astype(F32)
    hzf[...] = value
    hzs[...] = value.astype(BF16)
    h_z = scatter_z(hzs, 128, hrz)

    gfin[...] = sum_z(g_z, gzf, 256, grz).astype(BF16)
    g_swap = swap(gfin, gst.at[0:HW, :])

    hfin[...] = sum_z(h_z, hzf, 128, hrz).astype(BF16)
    h_pair = push(hfin, hp, core_peer)
    first = core == 0
    gr_out[arow, :] = jnp.where(first, hfin[:, 0:64], hfin[:, 64:128])
    h_pair.wait_recv()
    gr_out[rows(HA * far, HA), :] = jnp.where(first, hp[:, 0:64], hp[:, 64:128])

    g_swap()
    gst[HW:256, :] = jnp.zeros((256 - HW, 256), BF16)
    gs_out[...] = gst[...].T[:, 0:172]

    for copy in sent:
        copy.wait_send()
    for remote in swaps:
        @pl.when(moves)
        def _():
            remote.wait_send()


def local(activations, cotangent, small_weight, grow_rows, grow_cols):
    scale = float(32 * activations.shape[0]) ** -0.5
    bf, f32 = (lambda *s: pltpu.VMEM(s, BF16)), (lambda *s: pltpu.VMEM(s, F32))
    scratch = [
        bf(256, 256), bf(HW, 256), bf(4 * HW, 2048), bf(320, 128), bf(HA, 128), bf(4, 320, 512),
        bf(256, 768), bf(768, 256), bf(128, 384), bf(384, 128),
        bf(8, 128, 256), bf(7, 128, 256), bf(128, 256), bf(512, 2048),
        bf(7, FP, 256), bf(7, FP, 256), bf(FP, 2048), bf(512, 256), bf(256, 512),
        bf(7, FP, 256), bf(7, FP, 256), bf(FP, 2048),
        bf(256, 2048), bf(256, 2048), f32(256, 2048), bf(256, 2048), bf(3, HP, 1024),
        f32(HP, 1024), bf(HP, 1024), bf(3, HP, 256), bf(HP, 256), bf(HP, 2048),
        bf(2 * HW, 2048), bf(2 * HW, 2048), f32(2 * HW, 2048), bf(2 * HW, 2048), bf(3, HW, 1024),
        f32(HW, 1024), bf(HW, 1024), bf(3, HW, 256), bf(HW, 256), bf(256, 256),
        bf(4, HA, 512), bf(4, HA, 512), f32(4, HA, 512), bf(4, HA, 512), bf(3, HA, 512),
        f32(HA, 512), bf(HA, 512), bf(3, HA, 128), bf(HA, 128), bf(HA, 128),
        pltpu.SemaphoreType.DMA((NSEM,)), pltpu.SemaphoreType.DMA((NSEM,)), pltpu.SemaphoreType.DMA((4,)),
    ]
    vmem = pl.BlockSpec(memory_space=pltpu.VMEM)
    gr, gc, gs = pl.pallas_call(
        functools.partial(kernel, scale),
        out_shape=(
            jax.ShapeDtypeStruct((320, 64), BF16),
            jax.ShapeDtypeStruct((FP, 4 * HW), BF16),
            jax.ShapeDtypeStruct((256, 172), BF16),
        ),
        in_specs=[vmem] * 5,
        out_specs=(vmem,) * 3,
        scratch_shapes=scratch,
        compiler_params=pltpu.CompilerParams(
            collective_id=0, has_side_effects=True, vmem_limit_bytes=56 * 2**20
        ),
        cost_estimate=pl.CostEstimate(flops=3_700_000_000, bytes_accessed=3_000_000, transcendentals=110_592),
        name="grow",
    )(activations, cotangent, small_weight, grow_rows, grow_cols)
    gc = jnp.concatenate([gc[0:216, HW * KT[k]:HW * KT[k] + 172] for k in range(4)], axis=1)
    return gr, gc, gs


def solution(mesh):
    return jax.shard_map(
        local,
        mesh=mesh,
        in_specs=(
            P("col", "row"),
            P("row", "col"),
            P("row", "col"),
            P("row", "col"),
            P("col", "row"),
        ),
        out_specs=(P("row", "col"), P("col", "row"), P("row", "col")),
        check_vma=False,
    )
```

```python
import functools

import jax
import jax.numpy as jnp
from jax import lax
from jax.experimental import pallas as pl
from jax.experimental.pallas import tpu as pltpu
from jax.sharding import PartitionSpec as P

MESH = pl.DeviceIdType.MESH
F32 = jnp.float32
BF16 = jnp.bfloat16
HW = 176
HP = 128
FP = 224
LA = 384
NSEM = 256
KT = (0, 2, 1, 3)
CW = ((0, 96), (96, 80))
CP = ((0, 64), (64, 64))
CQ = ((0, 64), (64, 64))


def nn(a, b):
    return jnp.dot(a, b, preferred_element_type=F32)


def nt(a, b):
    return lax.dot_general(a, b, (((1,), (1,)), ((), ())), preferred_element_type=F32)


def lanes(start, size):
    return pl.ds(pl.multiple_of(start, 128), size)


def rows(start, size):
    return pl.ds(pl.multiple_of(start, 16), size)


def kernel(
    scale,
    act, cot, w, a, b,
    gr_out, gc_out, gs_out,
    wsend, wbuf, abuf, bp, bpt, actp, actt,
    ps, prcv, pblk, pbuf,
    cs, crcv, ct, delta, dt,
    bs, brcv, bt,
    qfar, qgot, qown, qhalf, qry, qyf, qys, qrx, qrz, qfin, qt,
    gfar, ggot, gown, ghalf, gry, gyf, gys, grx, grz,
    hfull, hs, hc, ho, hh, hry, hzf, hzs, hrz,
    ssem, rsem,
):
    r = lax.axis_index("row")
    c = lax.axis_index("col")
    x, zlo = r // 2, r % 2
    zhi, y, core = c // 8, (c // 2) % 4, c % 2
    yh, yl = y // 2, y % 2
    kt = 2 * core + yl
    far = 1 - core
    diag = zlo == yh
    stays = jnp.logical_and(x == zhi, diag)

    def row_peer(d):
        return ((r + d) % 8, c)

    def y_peer(d):
        return (r, zhi * 8 + ((y + d) % 4) * 2 + core)

    def z_peer(d):
        return (r, ((zhi + d) % 4) * 8 + y * 2 + core)

    core_peer = (r, c + 1 - 2 * core)

    def swap_target(j):
        return (zhi * 2 + yh, j * 8 + zlo * 4 + yl * 2 + core)

    def swap_source(s):
        return (s * 2 + yh, x * 8 + zlo * 4 + yl * 2 + core)

    def turn_peer(j):
        return (x * 2 + yh, j * 8 + zlo * 4 + yl * 2 + core)

    used = [0]
    sent = []

    def push(src, dst, device):
        i = used[0]
        used[0] += 1
        copy = pltpu.make_async_remote_copy(
            src_ref=src, dst_ref=dst, send_sem=ssem.at[i], recv_sem=rsem.at[i],
            device_id=device, device_id_type=MESH,
        )
        copy.start()
        sent.append((copy, None))
        return copy

    def push_when(cond, src, dst, device):
        i = used[0]
        used[0] += 1
        copy = pltpu.make_async_remote_copy(
            src_ref=src, dst_ref=dst, send_sem=ssem.at[i], recv_sem=rsem.at[i],
            device_id=device, device_id_type=MESH,
        )

        @pl.when(cond)
        def _():
            copy.start()

        sent.append((copy, cond))
        return copy

    def wait_all(copies):
        for copy in copies:
            copy.wait_recv()

    barrier = pltpu.get_barrier_semaphore()

    def greet(device):
        pl.semaphore_signal(barrier, inc=1, device_id=device, device_id_type=MESH)

    for d in range(1, 8):
        greet(row_peer(d))
    for d in range(1, 4):
        greet(y_peer(d))
        greet(z_peer(d))
    greet(core_peer)
    for s in range(4):
        pl.when(jnp.logical_not(jnp.logical_and(stays, x == s)))(lambda s=s: greet(swap_source(s)))
    for d in range(1, 4):
        greet(turn_peer((zhi + d) % 4))
    pl.when(jnp.logical_not(diag))(lambda: greet(turn_peer(zhi)))

    wsend[0:172, :] = w[...]
    wsend[172:HW, :] = jnp.zeros((HW - 172, 256), BF16)
    acol = rows(64 * (2 * yl + core), 64)
    abuf[yh, 0, acol, 0:320] = a[...]
    abuf[yh, 0, acol, 320:LA] = jnp.zeros((64, LA - 320), BF16)

    @pl.when(stays)
    def _():
        pl.semaphore_wait(barrier, 20)

    @pl.when(jnp.logical_and(diag, x != zhi))
    def _():
        pl.semaphore_wait(barrier, 21)

    @pl.when(jnp.logical_not(diag))
    def _():
        pl.semaphore_wait(barrier, 22)

    t_slot = lanes(1024 * zlo + 256 * x, 256)
    band = lanes(1024 * yh, 1024)

    def swap_gather(src, buf, height, chunk):
        off, size = chunk
        base = used[0]
        used[0] += 4
        at = rows(height * kt + off, size)
        for d in range(4):
            copy = pltpu.make_async_remote_copy(
                src_ref=src.at[off:off + size, :], dst_ref=buf.at[at, t_slot],
                send_sem=ssem.at[base + d], recv_sem=rsem.at[base + x],
                device_id=swap_target((zhi + d) % 4), device_id_type=MESH,
            )
            if d:
                copy.start()
                sent.append((copy, None))
            else:
                pl.when(jnp.logical_not(stays))(copy.start)
                sent.append((copy, jnp.logical_not(stays)))

        @pl.when(stays)
        def _():
            buf[at, t_slot] = src[off:off + size, :]

        def wait():
            for s in range(4):
                copy = pltpu.make_async_remote_copy(
                    src_ref=src.at[off:off + size, :], dst_ref=buf.at[at, t_slot],
                    send_sem=ssem.at[base], recv_sem=rsem.at[base + s],
                    device_id=core_peer, device_id_type=MESH,
                )
                pl.when(jnp.logical_not(jnp.logical_and(stays, x == s)))(copy.wait_recv)

        return wait

    def band_y(buf, height, chunk):
        off, size = chunk
        block = buf.at[rows(height * kt + off, size), band]
        return [push(block, block, y_peer(d)) for d in (1, 2, 3)]

    def band_core(buf, height, d):
        other = (y + 4 - d) % 4
        block = buf.at[rows(height * (2 * core + other % 2), height), lanes(1024 * (other // 2), 1024)]
        return push(block, block, core_peer)

    first = abuf.at[yh, 0, acol, :]
    a_z = [push(first, abuf.at[yh, 4 - d, acol, :], z_peer(d)) for d in (1, 2, 3)]
    a_y = [push(first, first, y_peer(d)) for d in (1, 2, 3)]
    w_sw = [swap_gather(wsend, wbuf, HW, chunk) for chunk in CW]
    a_core = [push(first, first, core_peer)]

    bp[...] = jnp.zeros_like(bp)
    for k in range(4):
        bp[0:216, HW * KT[k]:HW * KT[k] + 172] = b[:, 172 * k:172 * k + 172]
    actt[0:320, :] = act[...]
    actt[320:LA, :] = jnp.zeros((LA - 320, 128), BF16)
    actp[...] = actt[...].T

    wait_all(a_z)
    rest = abuf.at[yh, 1:4, acol, :]
    a_y2 = [push(rest, rest, y_peer(d)) for d in (1, 2, 3)]
    a_core.append(push(rest, rest, core_peer))

    w_sw[0]()
    w_y = [band_y(wbuf, HW, CW[0])]
    bpt[...] = bp[...].T

    for d in (1, 2, 3):
        a_y[d - 1].wait_recv()
        a_y2[d - 1].wait_recv()
        other = (y + 4 - d) % 4
        block = abuf.at[other // 2, :, rows(64 * (2 * (other % 2) + core), 64), :]
        a_core.append(push(block, block, core_peer))

    w_sw[1]()
    w_y.append(band_y(wbuf, HW, CW[1]))
    w_core = [band_core(wbuf, HW, 0)]
    wait_all(a_core)

    def p_term(peer):
        return nt(actp[...], abuf[peer % 2, (peer // 2 + 4 - zhi) % 4])

    p_rs = []
    for d in range(1, 8):
        ps[d - 1] = p_term((r + d) % 8).astype(BF16)
        p_rs.append(push(ps.at[d - 1], prcv.at[d - 1], row_peer(d)))
    total = p_term(r)
    dt[...] = jnp.zeros_like(dt)

    for d in (1, 2, 3):
        w_y[0][d - 1].wait_recv()
        w_y[1][d - 1].wait_recv()
        w_core.append(band_core(wbuf, HW, d))

    for d in range(7):
        p_rs[d].wait_recv()
        total = total + prcv[d].astype(F32)
    pblk[...] = total.astype(BF16)
    p_sw = [swap_gather(pblk, pbuf, HP, chunk) for chunk in CP]

    wait_all(w_core)

    def panel(peer):
        return lanes(1024 * (peer % 2) + 256 * (peer // 2), 256)

    own = panel(r)
    c_rs = []
    for d in range(1, 8):
        cs[d - 1] = nn(bp[0:FP, 0:4 * HW], wbuf[:, panel((r + d) % 8)]).astype(BF16)
        c_rs.append(push(cs.at[d - 1], crcv.at[d - 1], row_peer(d)))
    total = nn(bp[0:FP, 0:4 * HW], wbuf[:, own])

    p_sw[0]()
    p_y = [band_y(pbuf, HP, CP[0])]
    p_sw[1]()
    p_y.append(band_y(pbuf, HP, CP[1]))
    p_core = [band_core(pbuf, HP, 0)]

    for d in range(7):
        c_rs[d].wait_recv()
        total = total + crcv[d].astype(F32)
    ct[:, own] = total.astype(BF16)
    c_ag = [push(ct.at[:, own], ct.at[:, own], row_peer(d)) for d in range(1, 8)]

    for d in (1, 2, 3):
        p_y[0][d - 1].wait_recv()
        p_y[1][d - 1].wait_recv()
        p_core.append(band_core(pbuf, HP, d))
    wait_all(p_core)
    wait_all(c_ag)

    for k in range(4):
        t = KT[k]
        hidden = nt(ct[...], pbuf[HP * t:HP * t + HP, :])[0:216, :]
        s = 1.0 / (1.0 + jnp.exp(-hidden))
        grad = cot[:, HP * k:HP * k + HP].astype(F32) * s * (1.0 + hidden * (1.0 - s))
        dt[0:216, HP * t:HP * t + HP] = grad.astype(BF16)

    b_rs = []
    for d in range(1, 8):
        bs[d - 1] = nn(dt[0:FP, :], pbuf[:, panel((r + d) % 8)]).astype(BF16)
        b_rs.append(push(bs.at[d - 1], brcv.at[d - 1], row_peer(d)))
    delta[...] = dt[...].T

    def tiles(body):
        lax.fori_loop(0, 8, lambda i, _: (body(lanes(256 * i, 256)), 0)[1], 0)

    class Scatter:
        def __init__(self, height, chunks, far_ref, got, own_ref, half, ry, yf, ys, rx, rz):
            self.height, self.chunks = height, chunks
            self.far, self.got, self.own, self.half = far_ref, got, own_ref, half
            self.ry, self.yf, self.ys, self.rx, self.rz = ry, yf, ys, rx, rz
            n = len(chunks)
            self.core, self.y, self.x, self.z = [None] * n, [None] * n, [None] * n, [None] * n

        def to_core(self, i):
            off, size = self.chunks[i]
            self.core[i] = []
            for v in range(2):
                at = slice(self.height * v + off, self.height * v + off + size)
                self.core[i].append(push(self.far.at[at, :], self.got.at[at, :], core_peer))

        def to_y(self, i):
            off, size = self.chunks[i]
            wait_all(self.core[i])

            def add(at):
                for v in range(2):
                    part = slice(self.height * v + off, self.height * v + off + size)
                    value = self.own[part, at] + self.got[part, at].astype(F32)
                    self.own[part, at] = value
                    self.half[part, at] = value.astype(BF16)

            tiles(add)
            self.y[i] = []
            for d in (1, 2, 3):
                other = (y + d) % 4
                self.y[i].append(push(
                    self.half.at[rows(self.height * (other % 2) + off, size), lanes(1024 * (other // 2), 1024)],
                    self.ry.at[d - 1, off:off + size, :], y_peer(d)))

        def to_x(self, i):
            off, size = self.chunks[i]
            wait_all(self.y[i])
            for q in range(4):
                at = slice(256 * q, 256 * q + 256)
                value = self.own[rows(self.height * yl + off, size), lanes(1024 * yh + 256 * q, 256)]
                for d in range(3):
                    value = value + self.ry[d, off:off + size, at].astype(F32)
                self.ys[off:off + size, at] = value.astype(BF16)
            self.x[i] = [
                push(self.ys.at[off:off + size, lanes(256 * ((x + d) % 4), 256)],
                     self.rx.at[x, off:off + size, :], row_peer(2 * d))
                for d in (1, 2, 3)
            ]
            self.rx[x, off:off + size, :] = self.ys[off:off + size, lanes(256 * x, 256)]

        def to_z(self, i):
            off, size = self.chunks[i]
            wait_all(self.x[i])
            self.z[i] = [
                push(self.rx.at[(zhi + d) % 4, off:off + size, :], self.rz.at[zhi, off:off + size, :],
                     turn_peer((zhi + d) % 4))
                for d in (1, 2, 3)
            ]
            self.last = push_when(
                jnp.logical_not(diag), self.rx.at[zhi, off:off + size, :], self.rz.at[zhi, off:off + size, :],
                turn_peer(zhi))
            self.z[i].append(self.last)

            @pl.when(diag)
            def _():
                self.rz[zhi, off:off + size, :] = self.rx[zhi, off:off + size, :]

        def result(self, i):
            off, size = self.chunks[i]
            wait_all(self.z[i][:3])
            pl.when(jnp.logical_not(diag))(self.z[i][3].wait_recv)
            value = self.rz[0, off:off + size, :].astype(F32)
            for s in range(1, 4):
                value = value + self.rz[s, off:off + size, :].astype(F32)
            return value

    q = Scatter(HP, CQ, qfar, qgot, qown, qhalf, qry, qyf, qys, qrx, qrz)

    def q_far(at):
        qfar[:, at] = nn(delta[rows(2 * HP * far, 2 * HP), 0:FP], ct[:, at]).astype(BF16)

    def q_own(at):
        qown[:, at] = nn(delta[rows(2 * HP * core, 2 * HP), 0:FP], ct[:, at])

    tiles(q_far)
    q.to_core(0)
    q.to_core(1)
    tiles(q_own)
    total = nn(dt[0:FP, :], pbuf[:, own])
    q.to_y(0)
    q.to_y(1)

    for d in range(7):
        b_rs[d].wait_recv()
        total = total + brcv[d].astype(F32)
    bt[:, own] = (total * scale).astype(BF16)
    b_ag = [push(bt.at[:, own], bt.at[:, own], row_peer(d)) for d in range(1, 8)]

    q.to_x(0)
    q.to_x(1)
    q.to_z(0)

    g = Scatter(HW, CW, gfar, ggot, gown, ghalf, gry, gyf, gys, grx, grz)
    wait_all(b_ag)

    def g_far(at):
        gfar[:, at] = nn(bpt[rows(2 * HW * far, 2 * HW), 0:FP], bt[:, at]).astype(BF16)

    def g_own(at):
        gown[:, at] = nn(bpt[rows(2 * HW * core, 2 * HW), 0:FP], bt[:, at])

    tiles(g_far)
    g.to_core(0)
    g.to_core(1)
    q.to_z(1)
    tiles(g_own)
    g.to_y(0)
    g.to_y(1)

    for i, (off, size) in enumerate(CQ):
        qfin[off:off + size, :] = (q.result(i) * scale).astype(BF16)
    qt[:, own] = qfin[...]
    q_ag = [push(qfin, qt.at[:, own], row_peer(d)) for d in range(1, 8)]

    for k in range(4):
        t = KT[k]
        part = nt(bt[...], wbuf[HW * t:HW * t + HW, :])
        gc_out[:, 172 * k:172 * k + 172] = part[0:216, 0:172].astype(BF16)

    wait_all(q_ag)
    for v in range(8):
        hfull[v // 4, v % 4] = nn(qt[:, 256 * v:256 * v + 256].T, actp[...])
    for v in range(2):
        hs[:, :, 64 * v:64 * v + 64, :] = hfull[:, :, rows(64 * (2 * v + far), 64), :].astype(BF16)
    h_core = push(hs, hc, core_peer)
    g.to_x(0)
    h_core.wait_recv()
    for v in range(2):
        at = slice(64 * v, 64 * v + 64)
        value = hfull[:, :, rows(64 * (2 * v + core), 64), :] + hc[:, :, at, :].astype(F32)
        ho[:, :, at, :] = value
        hh[:, :, at, :] = value.astype(BF16)
    h_y = []
    for d in (1, 2, 3):
        other = (y + d) % 4
        h_y.append(push(hh.at[other // 2, :, rows(64 * (other % 2), 64), :], hry.at[d - 1], y_peer(d)))

    g.to_z(0)
    g.to_x(1)
    g.to_z(1)

    wait_all(h_y)
    value = ho[yh, :, rows(64 * yl, 64), :]
    for d in range(3):
        value = value + hry[d].astype(F32)
    hzf[...] = value
    hzs[...] = value.astype(BF16)
    h_z = [push(hzs.at[(zhi + d) % 4], hrz.at[d - 1], z_peer(d)) for d in (1, 2, 3)]

    gs_out[0:96, :] = g.result(0).astype(BF16)
    gs_out[96:172, :] = g.result(1)[0:76, :].astype(BF16)

    wait_all(h_z)
    value = hzf[zhi]
    for d in range(3):
        value = value + hrz[d].astype(F32)
    gr_out[...] = value[:, 0:320].astype(BF16)

    for copy, cond in sent:
        if cond is None:
            copy.wait_send()
        else:
            pl.when(cond)(copy.wait_send)


def local(activations, cotangent, small_weight, grow_rows, grow_cols):
    scale = float(32 * activations.shape[0]) ** -0.5
    bf, f32 = (lambda *s: pltpu.VMEM(s, BF16)), (lambda *s: pltpu.VMEM(s, F32))

    def scatter(height):
        return [
            bf(2 * height, 2048), bf(2 * height, 2048), f32(2 * height, 2048), bf(2 * height, 2048),
            bf(3, height, 1024), f32(height, 1024), bf(height, 1024), bf(4, height, 256), bf(4, height, 256),
        ]

    scratch = [
        bf(HW, 256), bf(4 * HW, 2048), bf(2, 4, 256, LA), bf(256, 768), bf(768, 256), bf(128, LA), bf(LA, 128),
        bf(7, 128, 256), bf(7, 128, 256), bf(128, 256), bf(512, 2048),
        bf(7, FP, 256), bf(7, FP, 256), bf(FP, 2048), bf(512, 256), bf(256, 512),
        bf(7, FP, 256), bf(7, FP, 256), bf(FP, 2048),
        *scatter(HP), bf(HP, 256), bf(HP, 2048),
        *scatter(HW),
        f32(2, 4, 256, LA), bf(2, 4, 128, LA), bf(2, 4, 128, LA), f32(2, 4, 128, LA), bf(2, 4, 128, LA),
        bf(3, 4, 64, LA), f32(4, 64, LA), bf(4, 64, LA), bf(3, 64, LA),
        pltpu.SemaphoreType.DMA((NSEM,)), pltpu.SemaphoreType.DMA((NSEM,)),
    ]
    vmem = pl.BlockSpec(memory_space=pltpu.VMEM)
    gr, gc, gs = pl.pallas_call(
        functools.partial(kernel, scale),
        out_shape=(
            jax.ShapeDtypeStruct((64, 320), BF16),
            jax.ShapeDtypeStruct((216, 688), BF16),
            jax.ShapeDtypeStruct((172, 256), BF16),
        ),
        in_specs=[vmem] * 5,
        out_specs=(vmem,) * 3,
        scratch_shapes=scratch,
        compiler_params=pltpu.CompilerParams(
            collective_id=0, has_side_effects=True, vmem_limit_bytes=56 * 2**20
        ),
        cost_estimate=pl.CostEstimate(flops=3_700_000_000, bytes_accessed=3_000_000, transcendentals=110_592),
        name="grow",
    )(activations.T, cotangent.T, small_weight.T, grow_rows.T, grow_cols)
    return gr.T, gc, gs.T


def solution(mesh):
    return jax.shard_map(
        local,
        mesh=mesh,
        in_specs=(
            P("col", "row"),
            P("row", "col"),
            P("row", "col"),
            P("row", "col"),
            P("col", "row"),
        ),
        out_specs=(P("row", "col"), P("col", "row"), P("row", "col")),
        check_vma=False,
    )
```

```python
import functools

import jax
import jax.numpy as jnp
from jax import lax
from jax.experimental import pallas as pl
from jax.experimental.pallas import tpu as pltpu
from jax.sharding import PartitionSpec as P

MESH = pl.DeviceIdType.MESH
F32 = jnp.float32
BF16 = jnp.bfloat16
HW = 176
HP = 128
FP = 224
HB = 4 * HW
LB = 768
LA = 384
NSEM = 256
KT = (0, 2, 1, 3)
CW = ((0, 96), (96, 80))


def nn(a, b):
    return jnp.dot(a, b, preferred_element_type=F32)


def nt(a, b):
    return lax.dot_general(a, b, (((1,), (1,)), ((), ())), preferred_element_type=F32)


def lanes(start, size):
    return pl.ds(pl.multiple_of(start, 128), size)


def rows(start, size):
    return pl.ds(pl.multiple_of(start, 16), size)


def kernel(
    scale,
    act_in, cot_in, w_in, a_in, b_in,
    gr_out, gc_out, gs_out,
    act, cot, w, a, b, gc,
    wpad, wbuf, bbuf, bbuft, apad, abuf, axb,
    pbuf, ct, delta, dt,
    bs, brcv, bt,
    qfar, qgot, qown, qhalf, qry, qyf, qys, qrz, qt,
    gfar, ggot, gown, ghalf, gry, gyf, gys, grz,
    gcs, gcx, gcf, gcn, gcz,
    hfull, hs, hc, hh, hy, hyf, hys, hr,
    ssem, rsem, lsem,
):
    r = lax.axis_index("row")
    c = lax.axis_index("col")
    x, zlo = r // 2, r % 2
    zhi, y, core = c // 8, (c // 2) % 4, c % 2
    yh, yl = y // 2, y % 2
    kt = 2 * core + yl
    kn = 2 * yl + core
    far = 1 - core
    near_row = r + 1 - 2 * zlo
    stays = jnp.logical_and(x == zhi, zlo == yh)

    def row_peer(d):
        return ((r + d) % 8, c)

    def y_peer(d):
        return (r, zhi * 8 + ((y + d) % 4) * 2 + core)

    def z_peer(d):
        return (r, ((zhi + d) % 4) * 8 + y * 2 + core)

    core_peer = (r, c + 1 - 2 * core)
    pair_peer = (r, zhi * 8 + (y + 1 - 2 * yl) * 2 + core)

    def swap_target(j):
        return (zhi * 2 + yh, j * 8 + zlo * 4 + yl * 2 + core)

    def swap_source(s):
        return (s * 2 + yh, x * 8 + zlo * 4 + yl * 2 + core)

    used = [0]
    sent = []

    def push(src, dst, device):
        i = used[0]
        used[0] += 1
        copy = pltpu.make_async_remote_copy(
            src_ref=src, dst_ref=dst, send_sem=ssem.at[i], recv_sem=rsem.at[i],
            device_id=device, device_id_type=MESH,
        )
        copy.start()
        sent.append((copy, None))
        return copy

    def wait_all(copies):
        for copy in copies:
            copy.wait_recv()

    barrier = pltpu.get_barrier_semaphore()

    def greet(device):
        pl.semaphore_signal(barrier, inc=1, device_id=device, device_id_type=MESH)

    for d in range(1, 8):
        greet(row_peer(d))
    for d in range(1, 4):
        greet(y_peer(d))
        greet(z_peer(d))
    greet(core_peer)
    for s in range(4):
        pl.when(jnp.logical_not(jnp.logical_and(stays, x == s)))(lambda s=s: greet(swap_source(s)))

    loads = [
        pltpu.make_async_copy(src, dst, lsem.at[i])
        for i, (src, dst) in enumerate(((act_in, act), (w_in, w), (a_in, a), (b_in, b), (cot_in, cot)))
    ]
    for load in loads:
        load.start()
    bbuf[:, FP:256, :] = jnp.zeros((8, 256 - FP, LB), BF16)
    bbuf[r] = jnp.zeros((256, LB), BF16)
    loads[1].wait()
    wpad[0:172, :] = w[...]
    wpad[172:HW, :] = jnp.zeros((HW - 172, 256), BF16)
    wbuf[zhi, rows(HW * (2 * y + core), HW), :] = wpad[...]
    loads[2].wait()
    apad[:, 0:320] = a[...]
    apad[:, 320:LA] = jnp.zeros((64, LA - 320), BF16)
    arow = rows(64 * kn, 64)
    abuf[arow, lanes(LA * r, LA)] = apad[...]
    loads[3].wait()
    for k in range(4):
        bbuf[r, 0:216, HW * k:HW * k + 172] = b[:, 172 * k:172 * k + 172]
    loads[0].wait()

    @pl.when(stays)
    def _():
        pl.semaphore_wait(barrier, 17)

    @pl.when(jnp.logical_not(stays))
    def _():
        pl.semaphore_wait(barrier, 18)

    class RowGather:
        def __init__(self, at):
            self.at = at

        def start(self):
            block = self.at(r)
            self.copies = [push(block, block, row_peer(2 * d)) for d in (1, 2, 3)]
            self.near = push(block, block, (near_row, c))

        def forward(self):
            self.near.wait_recv()
            block = self.at(near_row)
            self.copies += [push(block, block, row_peer(2 * d)) for d in (1, 2, 3)]

        def finish(self):
            wait_all(self.copies)

    class ColGather:
        def __init__(self, at, band):
            self.at, self.band = at, band
            self.y, self.core = [], []

        def start(self):
            block = self.at(zhi)
            self.z = [push(block, block, z_peer(d)) for d in (1, 2, 3)]

        def along_y(self, e):
            if e:
                self.z[e - 1].wait_recv()
            block = self.at((zhi + 4 - e) % 4)
            self.y.append([push(block, block, y_peer(d)) for d in (1, 2, 3)])

        def to_core(self, d):
            if d:
                for e in range(4):
                    self.y[e][d - 1].wait_recv()
            block = self.band((y + 4 - d) % 4)
            self.core.append(push(block, block, core_peer))

        def finish(self):
            wait_all(self.core)

    gather_w = ColGather(
        lambda z: wbuf.at[z, rows(HW * (2 * y + core), HW), :],
        lambda other: wbuf.at[:, rows(HW * (2 * other + core), HW), :])
    gather_a = RowGather(lambda row: abuf.at[arow, lanes(LA * row, LA)])
    gather_b = RowGather(lambda row: bbuf.at[row, 0:FP, :])

    base = used[0]
    used[0] += 4
    for d in range(4):
        copy = pltpu.make_async_remote_copy(
            src_ref=act, dst_ref=axb.at[zlo, x], send_sem=ssem.at[base + d], recv_sem=rsem.at[base + x],
            device_id=swap_target((zhi + d) % 4), device_id_type=MESH,
        )
        if d:
            copy.start()
            sent.append((copy, None))
        else:
            pl.when(jnp.logical_not(stays))(copy.start)
            sent.append((copy, jnp.logical_not(stays)))

    @pl.when(stays)
    def _():
        axb[zlo, x] = act[...]

    def act_wait():
        for s in range(4):
            copy = pltpu.make_async_remote_copy(
                src_ref=act, dst_ref=axb.at[zlo, x], send_sem=ssem.at[base], recv_sem=rsem.at[base + s],
                device_id=core_peer, device_id_type=MESH,
            )
            pl.when(jnp.logical_not(jnp.logical_and(stays, x == s)))(copy.wait_recv)

    gather_a.start()
    gather_w.start()
    gather_w.along_y(0)
    gather_b.start()
    gather_a.forward()
    gather_w.along_y(1)
    gather_w.along_y(2)
    gather_w.along_y(3)
    gather_a.finish()
    a_rows = abuf.at[arow, :]
    a_pair = push(a_rows, a_rows, pair_peer)
    a_core = [push(a_rows, a_rows, core_peer)]
    act_wait()
    act_y = push(axb.at[yh], axb.at[yh], y_peer(2))
    gather_b.forward()
    gather_w.to_core(0)
    a_pair.wait_recv()
    a_rows = abuf.at[rows(64 * (2 * (1 - yl) + core), 64), :]
    a_core.append(push(a_rows, a_rows, core_peer))
    dt[...] = jnp.zeros_like(dt)
    bt[...] = jnp.zeros_like(bt)
    wait_all(a_core)
    act_y.wait_recv()

    total = nn(abuf[:, 0:320], axb[0, 0])
    for v in range(1, 8):
        total = total + nn(abuf[:, LA * v:LA * v + 320], axb[v % 2, v // 2])
    prow = rows(HP * kt, HP)
    pbuf[prow, lanes(1024 * yh + 256 * zhi, 256)] = total.T.astype(BF16)
    gather_p = ColGather(
        lambda z: pbuf.at[prow, lanes(1024 * yh + 256 * z, 256)],
        lambda other: pbuf.at[rows(HP * (2 * core + other % 2), HP), lanes(1024 * (other // 2), 1024)])
    gather_p.start()
    gather_p.along_y(0)
    for d in (1, 2, 3):
        gather_w.to_core(d)
    for e in (1, 2, 3):
        gather_p.along_y(e)
    gather_p.to_core(0)
    gather_w.finish()

    def chain_term(row):
        return nn(bbuf[row, 0:FP, 0:HB], wbuf[row // 2, rows(HB * (row % 2), HB), :])

    total = chain_term(r) + chain_term(near_row)
    gather_b.finish()
    for d in (1, 2, 3):
        total = total + chain_term((r + 2 * d) % 8) + chain_term((near_row + 2 * d) % 8)

    def panel(row):
        return lanes(1024 * (row % 2) + 256 * (row // 2), 256)

    own = panel(r)
    ct[:, own] = total.astype(BF16)
    gather_c = RowGather(lambda row: ct.at[:, panel(row)])
    gather_c.start()
    gather_c.forward()
    for v in range(8):
        bbuft[v] = bbuf[v].T
    for d in (1, 2, 3):
        gather_p.to_core(d)
    gather_p.finish()
    loads[4].wait()
    gather_c.finish()

    for k in range(4):
        t = KT[k]
        hidden = nt(ct[...], pbuf[HP * t:HP * t + HP, :])[0:216, :]
        s = 1.0 / (1.0 + jnp.exp(-hidden))
        grad = cot[:, HP * k:HP * k + HP].astype(F32) * s * (1.0 + hidden * (1.0 - s))
        dt[0:216, HP * t:HP * t + HP] = grad.astype(BF16)

    b_rs = []
    for d in range(1, 8):
        bs[d - 1] = nn(dt[0:FP, :], pbuf[:, panel((r + d) % 8)]).astype(BF16)
        b_rs.append(push(bs.at[d - 1], brcv.at[d - 1], row_peer(d)))
    delta[...] = dt[...].T

    def tiles(body):
        lax.fori_loop(0, 8, lambda i, _: (body(lanes(256 * i, 256)), 0)[1], 0)

    def q_far(at):
        qfar[:, at] = nn(delta[rows(2 * HP * far, 2 * HP), 0:FP], ct[:, at]).astype(BF16)

    def q_own(at):
        qown[:, at] = nn(delta[rows(2 * HP * core, 2 * HP), 0:FP], ct[:, at])

    def q_sum(at):
        value = qown[:, at] + qgot[:, at].astype(F32)
        qown[:, at] = value
        qhalf[:, at] = value.astype(BF16)

    tiles(q_far)
    q_core = push(qfar, qgot, core_peer)
    tiles(q_own)
    back = nn(dt[0:FP, :], pbuf[:, own])
    q_core.wait_recv()
    tiles(q_sum)
    q_y = []
    for d in (1, 2, 3):
        other = (y + d) % 4
        q_y.append(push(
            qhalf.at[rows(HP * (other % 2), HP), lanes(1024 * (other // 2), 1024)], qry.at[d - 1], y_peer(d)))

    for d in range(7):
        b_rs[d].wait_recv()
        back = back + brcv[d].astype(F32)
    bt[0:FP, :] = (back * scale).astype(BF16)

    def cols_term(row):
        return nt(bt[0:FP, :], wbuf[row // 2, rows(HB * (row % 2), HB), :])

    gc_x = []
    for i, base_row in enumerate((near_row, r)):
        for d in (1, 2, 3):
            slot = 3 * i + d - 1
            gcs[slot, :, 0:HB] = cols_term((base_row + 2 * d) % 8).astype(BF16)
            gc_x.append(push(gcs.at[slot], gcx.at[slot], row_peer(2 * d)))

    def small_term(v, u, which):
        return nn(bbuft[v, rows(HW * (2 * u + which), HW), :], bt[...])

    for v in range(8):
        for u in range(2):
            gfar[v // 2, 2 * (v % 2) + u] = small_term(v, u, far).astype(BF16)
    g_core = push(gfar, ggot, core_peer)
    for v in range(8):
        for u in range(2):
            gown[v // 2, 2 * (v % 2) + u] = small_term(v, u, core)
    gcn[...] = cols_term(near_row)
    gcf[...] = cols_term(r)
    g_core.wait_recv()

    def g_sum(i, _):
        value = gown[i // 4, i % 4] + ggot[i // 4, i % 4].astype(F32)
        gown[i // 4, i % 4] = value
        ghalf[i // 4, i % 4] = value.astype(BF16)
        return 0

    lax.fori_loop(0, 16, g_sum, 0)
    g_y = [
        [push(ghalf.at[:, (y + d) % 4, off:off + size, :], gry.at[d - 1, :, off:off + size, :], y_peer(d))
         for d in (1, 2, 3)]
        for off, size in CW
    ]

    wait_all(q_y)
    for v in range(4):
        at = slice(256 * v, 256 * v + 256)
        value = qown[rows(HP * yl, HP), lanes(1024 * yh + 256 * v, 256)]
        for d in range(3):
            value = value + qry[d, :, at].astype(F32)
        qyf[:, at] = value
        qys[:, at] = value.astype(BF16)
    q_z = [push(qys.at[:, lanes(256 * ((zhi + d) % 4), 256)], qrz.at[d - 1], z_peer(d)) for d in (1, 2, 3)]

    wait_all(gc_x[0:3])
    value = gcn[...]
    for d in range(3):
        value = value + gcx[d, :, 0:HB].astype(F32)
    gcs[6, :, 0:HB] = value.astype(BF16)
    gc_z = push(gcs.at[6], gcz, (near_row, c))

    wait_all(q_z)
    value = qyf[:, lanes(256 * zhi, 256)]
    for d in range(3):
        value = value + qrz[d].astype(F32)
    qt[...] = (value * scale).T.astype(BF16)
    for v in range(8):
        hfull[v, :, 0:320] = nt(qt[...], axb[v % 2, v // 2])
    for u in range(2):
        hs[:, 64 * u:64 * u + 64, 0:320] = hfull[:, rows(64 * (2 * u + far), 64), 0:320].astype(BF16)
    h_core = push(hs, hc, core_peer)

    def small_z(i):
        off, size = CW[i]
        wait_all(g_y[i])
        for v in range(4):
            value = gown[v, y, off:off + size, :]
            for d in range(3):
                value = value + gry[d, v, off:off + size, :].astype(F32)
            gyf[v, off:off + size, :] = value
            gys[v, off:off + size, :] = value.astype(BF16)
        return [
            push(gys.at[(zhi + d) % 4, off:off + size, :], grz.at[d - 1, off:off + size, :], z_peer(d))
            for d in (1, 2, 3)
        ]

    h_core.wait_recv()
    for v in range(8):
        for u in range(2):
            at = slice(64 * u, 64 * u + 64)
            value = hfull[v, rows(64 * (2 * u + core), 64), 0:320] + hc[v, at, 0:320].astype(F32)
            hfull[v, rows(64 * (2 * u + core), 64), 0:320] = value
            hh[u, v, :, 0:320] = value.astype(BF16)
    h_pair = push(hh.at[1 - yl], hy, pair_peer)

    g_z = [small_z(0)]

    h_pair.wait_recv()
    for v in range(8):
        value = hfull[v, rows(64 * kn, 64), 0:320] + hy[v, :, 0:320].astype(F32)
        hyf[v, :, 0:320] = value
        hys[v, :, 0:320] = value.astype(BF16)
    h_r = [push(hys.at[(r + d) % 8], hr.at[d - 1], row_peer(d)) for d in range(1, 8)]

    g_z.append(small_z(1))

    wait_all(gc_x[3:6])
    value = gcf[...]
    for d in range(3):
        value = value + gcx[3 + d, :, 0:HB].astype(F32)
    gc_z.wait_recv()
    value = (value + gcz[:, 0:HB].astype(F32)).astype(BF16)
    for k in range(4):
        gc[:, 172 * k:172 * k + 172] = value[0:216, HW * k:HW * k + 172]
    gc_copy = pltpu.make_async_copy(gc, gc_out, lsem.at[5])
    gc_copy.start()

    wait_all(h_r)
    value = hyf[r, :, 0:320]
    for d in range(7):
        value = value + hr[d, :, 0:320].astype(F32)
    gr_out[...] = value.astype(BF16)

    for copies in g_z:
        wait_all(copies)
    value = gyf[zhi]
    for d in range(3):
        value = value + grz[d].astype(F32)
    gs_out[...] = value[0:172, :].astype(BF16)

    gc_copy.wait()
    for copy, cond in sent:
        if cond is None:
            copy.wait_send()
        else:
            pl.when(cond)(copy.wait_send)


def local(activations, cotangent, small_weight, grow_rows, grow_cols):
    scale = float(32 * activations.shape[0]) ** -0.5
    bf, f32 = (lambda *s: pltpu.VMEM(s, BF16)), (lambda *s: pltpu.VMEM(s, F32))
    scratch = [
        bf(320, 128), bf(216, 512), bf(172, 256), bf(64, 320), bf(216, 688), bf(216, 688),
        bf(HW, 256), bf(4, 8 * HW, 256), bf(8, 256, LB), bf(8, LB, 256), bf(64, LA), bf(256, 8 * LA),
        bf(2, 4, 320, 128),
        bf(512, 2048), bf(FP, 2048), bf(512, 256), bf(256, 512),
        bf(7, FP, 256), bf(7, FP, 256), bf(256, 256),
        bf(2 * HP, 2048), bf(2 * HP, 2048), f32(2 * HP, 2048), bf(2 * HP, 2048),
        bf(3, HP, 1024), f32(HP, 1024), bf(HP, 1024), bf(3, HP, 256), bf(256, 128),
        bf(4, 4, HW, 256), bf(4, 4, HW, 256), f32(4, 4, HW, 256), bf(4, 4, HW, 256),
        bf(3, 4, HW, 256), f32(4, HW, 256), bf(4, HW, 256), bf(3, HW, 256),
        bf(7, FP, LB), bf(6, FP, LB), f32(FP, HB), f32(FP, HB), bf(FP, LB),
        f32(8, 256, LA), bf(8, 128, LA), bf(8, 128, LA), bf(2, 8, 64, LA), bf(8, 64, LA),
        f32(8, 64, LA), bf(8, 64, LA), bf(7, 64, LA),
        pltpu.SemaphoreType.DMA((NSEM,)), pltpu.SemaphoreType.DMA((NSEM,)), pltpu.SemaphoreType.DMA((6,)),
    ]
    vmem, hbm = pl.BlockSpec(memory_space=pltpu.VMEM), pl.BlockSpec(memory_space=pl.ANY)
    gr, gc, gs = pl.pallas_call(
        functools.partial(kernel, scale),
        out_shape=(
            jax.ShapeDtypeStruct((64, 320), BF16),
            jax.ShapeDtypeStruct((216, 688), BF16),
            jax.ShapeDtypeStruct((172, 256), BF16),
        ),
        in_specs=[hbm] * 5,
        out_specs=(vmem, hbm, vmem),
        scratch_shapes=scratch,
        compiler_params=pltpu.CompilerParams(
            collective_id=0, has_side_effects=True, vmem_limit_bytes=60 * 2**20
        ),
        cost_estimate=pl.CostEstimate(flops=3_700_000_000, bytes_accessed=3_000_000, transcendentals=110_592),
        name="grow",
    )(activations.T, cotangent.T, small_weight.T, grow_rows.T, grow_cols)
    return gr.T, gc, gs.T


def solution(mesh):
    return jax.shard_map(
        local,
        mesh=mesh,
        in_specs=(
            P("col", "row"),
            P("row", "col"),
            P("row", "col"),
            P("row", "col"),
            P("col", "row"),
        ),
        out_specs=(P("row", "col"), P("col", "row"), P("row", "col")),
        check_vma=False,
    )
```

```python
import functools

import jax
import jax.numpy as jnp
from jax import lax
from jax.experimental import pallas as pl
from jax.experimental.pallas import tpu as pltpu
from jax.sharding import PartitionSpec as P

MESH = pl.DeviceIdType.MESH
F32 = jnp.float32
BF16 = jnp.bfloat16
HW = 176
HP = 128
FP = 224
HB = 4 * HW
LB = 768
LA = 384
NSEM = 256
KT = (0, 2, 1, 3)
CW = ((0, 96), (96, 80))
CQ = ((0, 64), (64, 64))


def nn(a, b):
    return jnp.dot(a, b, preferred_element_type=F32)


def nt(a, b):
    return lax.dot_general(a, b, (((1,), (1,)), ((), ())), preferred_element_type=F32)


def lanes(start, size):
    return pl.ds(pl.multiple_of(start, 128), size)


def rows(start, size):
    return pl.ds(pl.multiple_of(start, 16), size)


def kernel(
    scale,
    act_in, cot_in, w_in, a_in, b_in,
    gr_out, gc_out, gs_out,
    act, cot, w, a, b, gc,
    wpad, wbuf, bbuf, bbuft, apad, abuf, axb,
    pbuf, ct, delta, dt,
    bs, brcv, bt,
    qfar, qgot, qown, qhalf, qry, qyf, qys, qrz, qt,
    gfar, ggot, gown, ghalf, gry, gyf, gys, grz,
    gcs, gcx, gcr, gce, gcf, gcn, gcz,
    hfull, hs, hc, hh, hyf, hr, hp, hq, hy,
    ssem, rsem, lsem,
):
    r = lax.axis_index("row")
    c = lax.axis_index("col")
    x, zlo = r // 2, r % 2
    zhi, y, core = c // 8, (c // 2) % 4, c % 2
    yh, yl = y // 2, y % 2
    kt = 2 * core + yl
    kn = 2 * yl + core
    far = 1 - core
    near_row = r + 1 - 2 * zlo
    stays = jnp.logical_and(x == zhi, zlo == yh)

    def row_peer(d):
        return ((r + d) % 8, c)

    def y_peer(d):
        return (r, zhi * 8 + ((y + d) % 4) * 2 + core)

    def z_peer(d):
        return (r, ((zhi + d) % 4) * 8 + y * 2 + core)

    core_peer = (r, c + 1 - 2 * core)
    pair_peer = (r, zhi * 8 + (y + 1 - 2 * yl) * 2 + core)

    def swap_target(j):
        return (zhi * 2 + yh, j * 8 + zlo * 4 + yl * 2 + core)

    def swap_source(s):
        return (s * 2 + yh, x * 8 + zlo * 4 + yl * 2 + core)

    used = [0]
    sent = []

    def push(src, dst, device):
        i = used[0]
        used[0] += 1
        copy = pltpu.make_async_remote_copy(
            src_ref=src, dst_ref=dst, send_sem=ssem.at[i], recv_sem=rsem.at[i],
            device_id=device, device_id_type=MESH,
        )
        copy.start()
        sent.append((copy, None))
        return copy

    def wait_all(copies):
        for copy in copies:
            copy.wait_recv()

    barrier = pltpu.get_barrier_semaphore()

    def greet(device):
        pl.semaphore_signal(barrier, inc=1, device_id=device, device_id_type=MESH)

    for d in range(1, 8):
        greet(row_peer(d))
    for d in range(1, 4):
        greet(y_peer(d))
        greet(z_peer(d))
    greet(core_peer)
    for s in range(4):
        pl.when(jnp.logical_not(jnp.logical_and(stays, x == s)))(lambda s=s: greet(swap_source(s)))

    loads = [
        pltpu.make_async_copy(src, dst, lsem.at[i])
        for i, (src, dst) in enumerate(((act_in, act), (w_in, w), (a_in, a), (b_in, b), (cot_in, cot)))
    ]
    for load in loads:
        load.start()
    bbuf[:, FP:256, :] = jnp.zeros((8, 256 - FP, LB), BF16)
    bbuf[r] = jnp.zeros((256, LB), BF16)
    loads[1].wait()
    wpad[0:172, :] = w[...]
    wpad[172:HW, :] = jnp.zeros((HW - 172, 256), BF16)
    wbuf[zhi, rows(HW * (2 * y + core), HW), :] = wpad[...]
    loads[2].wait()
    apad[:, 0:320] = a[...]
    apad[:, 320:LA] = jnp.zeros((64, LA - 320), BF16)
    arow = rows(64 * kt, 64)
    acore = rows(128 * core, 128)
    abuf[arow, lanes(LA * r, LA)] = apad[...]

    loads[3].wait()
    for k in range(4):
        bbuf[r, 0:216, HW * k:HW * k + 172] = b[:, 172 * k:172 * k + 172]
    loads[0].wait()

    @pl.when(stays)
    def _():
        pl.semaphore_wait(barrier, 17)

    @pl.when(jnp.logical_not(stays))
    def _():
        pl.semaphore_wait(barrier, 18)

    class RowGather:
        def __init__(self, at):
            self.at = at

        def start(self):
            block = self.at(r)
            self.copies = [push(block, block, row_peer(2 * d)) for d in (1, 2, 3)]

        def start_near(self):
            block = self.at(r)
            self.near = push(block, block, (near_row, c))

        def forward(self):
            self.near.wait_recv()
            block = self.at(near_row)
            self.copies += [push(block, block, row_peer(2 * d)) for d in (1, 2, 3)]

        def finish(self):
            wait_all(self.copies)

    class RingGather:
        def __init__(self, row, whole, half):
            self.row, self.whole, self.half = row, whole, half

        def start(self):
            block = self.whole(self.row)
            self.ahead = push(block, block, row_peer(2))
            self.behind = push(block, block, row_peer(6))

        def relay(self):
            self.ahead.wait_recv()
            block = self.half((self.row + 6) % 8, 0)
            self.rest = [push(block, block, row_peer(2))]
            self.behind.wait_recv()
            block = self.half((self.row + 2) % 8, 1)
            self.rest.append(push(block, block, row_peer(6)))

        def finish(self):
            wait_all(self.rest)

    class ColGather:
        def __init__(self, at, band):
            self.at, self.band = at, band
            self.y, self.core = [], []

        def start(self):
            block = self.at(zhi)
            self.z = [push(block, block, z_peer(d)) for d in (1, 2, 3)]

        def along_y(self, e):
            if e:
                self.z[e - 1].wait_recv()
            block = self.at((zhi + 4 - e) % 4)
            self.y.append([push(block, block, y_peer(d)) for d in (1, 2, 3)])

        def to_core(self, d):
            if d:
                for e in range(4):
                    self.y[e][d - 1].wait_recv()
            block = self.band((y + 4 - d) % 4)
            self.core.append(push(block, block, core_peer))

        def finish(self):
            wait_all(self.core)

    gather_w = ColGather(
        lambda z: wbuf.at[z, rows(HW * (2 * y + core), HW), :],
        lambda other: wbuf.at[:, rows(HW * (2 * other + core), HW), :])
    gather_a = RowGather(lambda row: abuf.at[acore, lanes(LA * row, LA)])
    b_parts = (lambda row: bbuf.at[row, 0:FP, :]), (lambda row, i: bbuf.at[row, 112 * i:112 * i + 112, :])
    gather_b = RingGather(r, *b_parts)
    gather_bn = RingGather(near_row, *b_parts)
    b_near = push(bbuf.at[r, 0:FP, :], bbuf.at[r, 0:FP, :], (near_row, c))
    gather_b.start()


    base = used[0]
    used[0] += 4
    for d in range(4):
        copy = pltpu.make_async_remote_copy(
            src_ref=act, dst_ref=axb.at[zlo, x], send_sem=ssem.at[base + d], recv_sem=rsem.at[base + x],
            device_id=swap_target((zhi + d) % 4), device_id_type=MESH,
        )
        if d:
            copy.start()
            sent.append((copy, None))
        else:
            pl.when(jnp.logical_not(stays))(copy.start)
            sent.append((copy, jnp.logical_not(stays)))

    @pl.when(stays)
    def _():
        axb[zlo, x] = act[...]

    def act_wait():
        for s in range(4):
            copy = pltpu.make_async_remote_copy(
                src_ref=act, dst_ref=axb.at[zlo, x], send_sem=ssem.at[base], recv_sem=rsem.at[base + s],
                device_id=core_peer, device_id_type=MESH,
            )
            pl.when(jnp.logical_not(jnp.logical_and(stays, x == s)))(copy.wait_recv)

    a_block = abuf.at[arow, lanes(LA * r, LA)]
    a_pair = push(a_block, a_block, pair_peer)
    gather_w.along_y(0)
    gather_b.relay()
    a_pair.wait_recv()
    gather_a.start_near()
    gather_a.start()
    b_near.wait_recv()
    gather_bn.start()
    dt[...] = jnp.zeros_like(dt)
    bt[...] = jnp.zeros_like(bt)
    act_wait()
    act_y = push(axb.at[yh], axb.at[yh], y_peer(2))
    gather_w.start()
    gather_a.forward()
    gather_bn.relay()
    for e in (1, 2, 3):
        gather_w.along_y(e)
    gather_a.finish()
    a_core = push(abuf.at[acore, :], abuf.at[acore, :], core_peer)

    a_core.wait_recv()
    act_y.wait_recv()
    total = nn(abuf[:, 0:320], axb[0, 0])
    for v in range(1, 8):
        total = total + nn(abuf[:, LA * v:LA * v + 320], axb[v % 2, v // 2])
    prow = rows(HP * kt, HP)
    pbuf[prow, lanes(1024 * yh + 256 * zhi, 256)] = jnp.concatenate(
        [total[0:64], total[128:192], total[64:128], total[192:256]], axis=0).T.astype(BF16)
    gather_p = ColGather(
        lambda z: pbuf.at[prow, lanes(1024 * yh + 256 * z, 256)],
        lambda other: pbuf.at[rows(HP * (2 * core + other % 2), HP), lanes(1024 * (other // 2), 1024)])
    gather_p.start()
    gather_p.along_y(0)
    for d in range(4):
        gather_w.to_core(d)
    for e in (1, 2, 3):
        gather_p.along_y(e)
    gather_p.to_core(0)

    def chain_term(row):
        return nn(bbuf[row, 0:FP, 0:HB], wbuf[row // 2, rows(HB * (row % 2), HB), :])

    def panel(row):
        return lanes(1024 * (row % 2) + 256 * (row // 2), 256)

    own = panel(r)
    gather_w.finish()
    total = chain_term(r) + chain_term(near_row)
    gather_b.finish()
    gather_bn.finish()
    for d in (1, 2, 3):
        total = total + chain_term((r + 2 * d) % 8) + chain_term((near_row + 2 * d) % 8)
    ct[:, own] = total.astype(BF16)
    gather_c = RowGather(lambda row: ct.at[:, panel(row)])
    gather_c.start_near()
    gather_c.start()

    gather_c.forward()
    for v in range(8):
        bbuft[v] = bbuf[v].T
    for d in (1, 2, 3):
        gather_p.to_core(d)
    gather_p.finish()
    loads[4].wait()
    gather_c.finish()

    for k in range(4):
        t = KT[k]
        hidden = nt(ct[...], pbuf[HP * t:HP * t + HP, :])[0:216, :]
        s = 1.0 / (1.0 + jnp.exp(-hidden))
        grad = cot[:, HP * k:HP * k + HP].astype(F32) * s * (1.0 + hidden * (1.0 - s))
        dt[0:216, HP * t:HP * t + HP] = grad.astype(BF16)

    delta[...] = dt[...].T

    def tiles(body):
        lax.fori_loop(0, 8, lambda i, _: (body(lanes(256 * i, 256)), 0)[1], 0)

    def q_far(at):
        qfar[:, at] = nn(delta[rows(2 * HP * far, 2 * HP), 0:FP], ct[:, at]).astype(BF16)

    def q_sum(at):
        value = nn(delta[rows(2 * HP * core, 2 * HP), 0:FP], ct[:, at]) + qgot[:, at].astype(F32)
        qown[:, at] = value
        qhalf[:, at] = value.astype(BF16)

    tiles(q_far)
    q_core = push(qfar, qgot, core_peer)

    b_rs = []
    for d in range(1, 8):
        bs[d - 1] = nn(dt[0:FP, :], pbuf[:, panel((r + d) % 8)]).astype(BF16)
        b_rs.append(push(bs.at[d - 1], brcv.at[d - 1], row_peer(d)))
    back = nn(dt[0:FP, :], pbuf[:, own])

    q_core.wait_recv()
    tiles(q_sum)
    q_y = [
        [push(qhalf.at[rows(HP * ((y + d) % 2) + off, size), lanes(1024 * (((y + d) % 4) // 2), 1024)],
              qry.at[d - 1, off:off + size, :], y_peer(d)) for d in (1, 2, 3)]
        for off, size in CQ
    ]

    for d in range(7):
        b_rs[d].wait_recv()
        back = back + brcv[d].astype(F32)
    bt[0:FP, :] = (back * scale).astype(BF16)

    def cols_term(row):
        return nt(bt[0:FP, :], wbuf[row // 2, rows(HB * (row % 2), HB), :])

    class RingSum:
        def __init__(self, i, row):
            self.i, self.row = i, row

        def start(self):
            self.relayed = []
            for d, slot in ((2, 0), (1, 1), (3, 2)):
                gcs[self.i, slot, :, 0:HB] = cols_term((self.row + 2 * d) % 8).astype(BF16)
                if d == 2:
                    for h, peer in ((0, 2), (1, 6)):
                        self.relayed.append(push(
                            gcs.at[self.i, 0, 112 * h:112 * h + 112, :], gcr.at[self.i, h], row_peer(peer)))
            self.direct = []
            for slot, h, peer in ((1, 1, 2), (2, 0, 6)):
                block = slice(112 * h, 112 * h + 112)
                self.direct.append(push(
                    gcs.at[self.i, slot, block, :], gcx.at[self.i, slot - 1, block, :], row_peer(peer)))

        def relay(self):
            for slot, h, peer in ((1, 0, 2), (2, 1, 6)):
                block = slice(112 * h, 112 * h + 112)
                self.relayed[h].wait_recv()
                value = gcs[self.i, slot, block, 0:HB].astype(F32) + gcr[self.i, h, :, 0:HB].astype(F32)
                gcs[self.i, slot, block, 0:HB] = value.astype(BF16)
                self.direct.append(push(
                    gcs.at[self.i, slot, block, :], gcx.at[self.i, slot - 1, block, :], row_peer(peer)))

        def result(self, value):
            wait_all(self.direct)
            return value + gcx[self.i, 0, :, 0:HB].astype(F32) + gcx[self.i, 1, :, 0:HB].astype(F32)

    cols_near, cols_own = RingSum(0, near_row), RingSum(1, r)

    def small_term(v, u, which):
        return nn(bbuft[v, rows(HW * (2 * u + which), HW), :], bt[...])

    for v in range(8):
        for u in range(2):
            gfar[v // 2, 2 * (v % 2) + u] = small_term(v, u, far).astype(BF16)
    g_core = push(gfar, ggot, core_peer)

    q_z = []
    for i, (off, size) in enumerate(CQ):
        wait_all(q_y[i])
        part = slice(off, off + size)
        for v in range(4):
            at = slice(256 * v, 256 * v + 256)
            value = qown[rows(HP * yl + off, size), lanes(1024 * yh + 256 * v, 256)]
            for d in range(3):
                value = value + qry[d, part, at].astype(F32)
            qyf[part, at] = value
            qys[part, at] = value.astype(BF16)
        q_z.append([
            push(qys.at[part, lanes(256 * ((zhi + d) % 4), 256)], qrz.at[d - 1, part, :], z_peer(d))
            for d in (1, 2, 3)
        ])

    cols_near.start()
    g_core.wait_recv()
    for v in range(8):
        for u in range(2):
            at = v // 2, 2 * (v % 2) + u
            value = small_term(v, u, core) + ggot[at].astype(F32)
            gown[at] = value
            ghalf[at] = value.astype(BF16)

    def small_y(i):
        off, size = CW[i]
        return [
            push(ghalf.at[:, (y + d) % 4, off:off + size, :], gry.at[d - 1, :, off:off + size, :], y_peer(d))
            for d in (1, 2, 3)
        ]

    g_y = [small_y(0), small_y(1)]

    for copies in q_z:
        wait_all(copies)
    value = qyf[:, lanes(256 * zhi, 256)]
    for d in range(3):
        value = value + qrz[d].astype(F32)
    qt[...] = (value * scale).T.astype(BF16)
    for v in range(8):
        hfull[v, :, 0:320] = nt(qt[...], axb[v % 2, v // 2])
    for u in range(2):
        hs[:, 64 * u:64 * u + 64, 0:320] = hfull[:, rows(64 * (2 * u + far), 64), 0:320].astype(BF16)
    h_core = push(hs, hc, core_peer)
    cols_near.relay()
    h_core.wait_recv()
    for v in range(8):
        for u in range(2):
            value = hfull[v, rows(64 * (2 * u + core), 64), 0:320] + hc[v, 64 * u:64 * u + 64, 0:320].astype(F32)
            hyf[v, u, :, 0:320] = value
            hh[v, u, :, 0:320] = value.astype(BF16)
    h_r = [push(hh.at[(r + d) % 8], hr.at[d - 1], row_peer(d)) for d in range(1, 8)]

    cols_own.start()
    gcn[...] = cols_term(near_row)
    gcf[...] = cols_term(r)

    def small_z(i):
        off, size = CW[i]
        wait_all(g_y[i])
        for v in range(4):
            value = gown[v, y, off:off + size, :]
            for d in range(3):
                value = value + gry[d, v, off:off + size, :].astype(F32)
            gyf[v, off:off + size, :] = value
            gys[v, off:off + size, :] = value.astype(BF16)
        return [
            push(gys.at[(zhi + d) % 4, off:off + size, :], grz.at[d - 1, off:off + size, :], z_peer(d))
            for d in (1, 2, 3)
        ]

    g_z = [small_z(0)]

    gce[:, 0:HB] = cols_near.result(gcn[...]).astype(BF16)
    gc_z = push(gce, gcz, (near_row, c))

    wait_all(h_r)
    for u in range(2):
        value = hyf[r, u, :, 0:320]
        for d in range(7):
            value = value + hr[d, u, :, 0:320].astype(F32)
        hp[u, :, 0:320] = value
        hq[u, :, 0:320] = value.astype(BF16)
    h_pair = push(hq.at[1 - yl], hy, pair_peer)
    g_z.append(small_z(1))
    cols_own.relay()

    value = cols_own.result(gcf[...])
    gc_z.wait_recv()
    value = (value + gcz[:, 0:HB].astype(F32)).astype(BF16)
    for k in range(4):
        gc[:, 172 * k:172 * k + 172] = value[0:216, HW * k:HW * k + 172]
    gc_copy = pltpu.make_async_copy(gc, gc_out, lsem.at[5])
    gc_copy.start()

    h_pair.wait_recv()
    gr_out[...] = (hp[yl, :, 0:320] + hy[:, 0:320].astype(F32)).astype(BF16)

    for copies in g_z:
        wait_all(copies)
    value = gyf[zhi]
    for d in range(3):
        value = value + grz[d].astype(F32)
    gs_out[...] = value[0:172, :].astype(BF16)

    gc_copy.wait()
    for copy, cond in sent:
        if cond is None:
            copy.wait_send()
        else:
            pl.when(cond)(copy.wait_send)


def store(gr, gc, gs, gr_out, gc_out, gs_out):
    gr_out[...] = gr[...]
    gc_out[...] = gc[...]
    gs_out[...] = gs[...]


def local(activations, cotangent, small_weight, grow_rows, grow_cols):
    scale = float(32 * activations.shape[0]) ** -0.5
    bf, f32 = (lambda *s: pltpu.VMEM(s, BF16)), (lambda *s: pltpu.VMEM(s, F32))
    scratch = [
        bf(320, 128), bf(216, 512), bf(172, 256), bf(64, 320), bf(216, 688), bf(216, 688),
        bf(HW, 256), bf(4, 8 * HW, 256), bf(8, 256, LB), bf(8, LB, 256), bf(64, LA), bf(256, 8 * LA),
        bf(2, 4, 320, 128),
        bf(512, 2048), bf(FP, 2048), bf(512, 256), bf(256, 512),
        bf(7, FP, 256), bf(7, FP, 256), bf(256, 256),
        bf(2 * HP, 2048), bf(2 * HP, 2048), f32(2 * HP, 2048), bf(2 * HP, 2048),
        bf(3, HP, 1024), f32(HP, 1024), bf(HP, 1024), bf(3, HP, 256), bf(256, 128),
        bf(4, 4, HW, 256), bf(4, 4, HW, 256), f32(4, 4, HW, 256), bf(4, 4, HW, 256),
        bf(3, 4, HW, 256), f32(4, HW, 256), bf(4, HW, 256), bf(3, HW, 256),
        bf(2, 3, FP, LB), bf(2, 2, FP, LB), bf(2, 2, 112, LB), bf(FP, LB), f32(FP, HB), f32(FP, HB), bf(FP, LB),
        f32(8, 256, LA), bf(8, 128, LA), bf(8, 128, LA), bf(8, 2, 64, LA), f32(8, 2, 64, LA),
        bf(7, 2, 64, LA), f32(2, 64, LA), bf(2, 64, LA), bf(64, LA),
        pltpu.SemaphoreType.DMA((NSEM,)), pltpu.SemaphoreType.DMA((NSEM,)), pltpu.SemaphoreType.DMA((6,)),
    ]
    vmem, hbm = pl.BlockSpec(memory_space=pltpu.VMEM), pl.BlockSpec(memory_space=pl.ANY)
    out_shape = (
        jax.ShapeDtypeStruct((64, 320), BF16),
        jax.ShapeDtypeStruct((216, 688), BF16),
        jax.ShapeDtypeStruct((172, 256), BF16),
    )
    results = pl.pallas_call(
        functools.partial(kernel, scale),
        out_shape=out_shape,
        in_specs=[hbm] * 5,
        out_specs=(vmem, hbm, vmem),
        scratch_shapes=scratch,
        compiler_params=pltpu.CompilerParams(
            collective_id=0, has_side_effects=True, vmem_limit_bytes=60 * 2**20
        ),
        cost_estimate=pl.CostEstimate(flops=3_700_000_000, bytes_accessed=3_000_000, transcendentals=110_592),
        name="grow",
    )(activations.T, cotangent.T, small_weight.T, grow_rows.T, grow_cols)
    gr, gc, gs = pl.pallas_call(
        store,
        out_shape=out_shape,
        in_specs=[vmem] * 3,
        out_specs=(vmem,) * 3,
        name="store",
    )(*results)
    return gr.T, gc, gs.T


def solution(mesh):
    return jax.shard_map(
        local,
        mesh=mesh,
        in_specs=(
            P("col", "row"),
            P("row", "col"),
            P("row", "col"),
            P("row", "col"),
            P("col", "row"),
        ),
        out_specs=(P("row", "col"), P("col", "row"), P("row", "col")),
        check_vma=False,
    )
```

```python
import functools

import jax
import jax.numpy as jnp
from jax import lax
from jax.experimental import pallas as pl
from jax.experimental.pallas import tpu as pltpu
from jax.sharding import PartitionSpec as P

MESH = pl.DeviceIdType.MESH
F32 = jnp.float32
BF16 = jnp.bfloat16
HW = 176
HP = 128
FP = 224
HB = 4 * HW
LB = 768
LA = 384
NSEM = 256
KT = (0, 2, 1, 3)
CW = ((0, 96), (96, 80))
CQ = ((0, 64), (64, 64))


def nn(a, b):
    return jnp.dot(a, b, preferred_element_type=F32)


def nt(a, b):
    return lax.dot_general(a, b, (((1,), (1,)), ((), ())), preferred_element_type=F32)


def lanes(start, size):
    return pl.ds(pl.multiple_of(start, 128), size)


def rows(start, size):
    return pl.ds(pl.multiple_of(start, 16), size)


def kernel(
    scale,
    act_in, cot_in, w_in, a_in, b_in,
    gr_out, gc_out, gs_out,
    act, cot, w, a, b, gc,
    wpad, wbuf, bbuf, bbuft, apad, abuf, axb,
    pbuf, ct, delta, dt,
    bs, brcv, bt,
    qfar, qgot, qown, qhalf, qry, qyf, qys, qrz, qt,
    gfar, ggot, gown, ghalf, gry, gyf, gys, grz,
    gcs, gcx, gcr, gce, gcf, gcn, gcz,
    hfull, hs, hc, hh, hyf, hr, hp, hq, hy,
    ssem, rsem, lsem,
):
    r = lax.axis_index("row")
    c = lax.axis_index("col")
    x, zlo = r // 2, r % 2
    zhi, y, core = c // 8, (c // 2) % 4, c % 2
    yh, yl = y // 2, y % 2
    kt = 2 * core + yl
    kn = 2 * yl + core
    far = 1 - core
    near_row = r + 1 - 2 * zlo
    stays = jnp.logical_and(x == zhi, zlo == yh)

    def row_peer(d):
        return ((r + d) % 8, c)

    def y_peer(d):
        return (r, zhi * 8 + ((y + d) % 4) * 2 + core)

    def z_peer(d):
        return (r, ((zhi + d) % 4) * 8 + y * 2 + core)

    core_peer = (r, c + 1 - 2 * core)
    pair_peer = (r, zhi * 8 + (y + 1 - 2 * yl) * 2 + core)

    def swap_target(j):
        return (zhi * 2 + yh, j * 8 + zlo * 4 + yl * 2 + core)

    def swap_source(s):
        return (s * 2 + yh, x * 8 + zlo * 4 + yl * 2 + core)

    used = [0]
    sent = []

    def push(src, dst, device):
        i = used[0]
        used[0] += 1
        copy = pltpu.make_async_remote_copy(
            src_ref=src, dst_ref=dst, send_sem=ssem.at[i], recv_sem=rsem.at[i],
            device_id=device, device_id_type=MESH,
        )
        copy.start()
        sent.append((copy, None))
        return copy

    def wait_all(copies):
        for copy in copies:
            copy.wait_recv()

    barrier = pltpu.get_barrier_semaphore()

    def greet(device):
        pl.semaphore_signal(barrier, inc=1, device_id=device, device_id_type=MESH)

    for d in range(1, 8):
        greet(row_peer(d))
    for d in range(1, 4):
        greet(y_peer(d))
        greet(z_peer(d))
    greet(core_peer)
    for s in range(4):
        pl.when(jnp.logical_not(jnp.logical_and(stays, x == s)))(lambda s=s: greet(swap_source(s)))

    loads = [
        pltpu.make_async_copy(src, dst, lsem.at[i])
        for i, (src, dst) in enumerate(((act_in, act), (w_in, w), (a_in, a), (b_in, b), (cot_in, cot)))
    ]
    for load in loads:
        load.start()
    bbuf[:, FP:256, :] = jnp.zeros((8, 256 - FP, LB), BF16)
    bbuf[r] = jnp.zeros((256, LB), BF16)
    loads[1].wait()
    wpad[0:172, :] = w[...]
    wpad[172:HW, :] = jnp.zeros((HW - 172, 256), BF16)
    wbuf[0, rows(HW * (2 * y + core), HW), :] = wpad[...]
    loads[2].wait()
    apad[:, 0:320] = a[...]
    apad[:, 320:LA] = jnp.zeros((64, LA - 320), BF16)
    arow = rows(64 * kt, 64)
    acore = rows(128 * core, 128)
    abuf[arow, lanes(LA * r, LA)] = apad[...]

    loads[3].wait()
    for k in range(4):
        bbuf[r, 0:216, HW * k:HW * k + 172] = b[:, 172 * k:172 * k + 172]
    loads[0].wait()

    @pl.when(stays)
    def _():
        pl.semaphore_wait(barrier, 17)

    @pl.when(jnp.logical_not(stays))
    def _():
        pl.semaphore_wait(barrier, 18)

    class RowGather:
        def __init__(self, at):
            self.at = at

        def start(self):
            block = self.at(r)
            self.copies = [push(block, block, row_peer(2 * d)) for d in (1, 2, 3)]

        def start_near(self):
            block = self.at(r)
            self.near = push(block, block, (near_row, c))

        def forward(self):
            self.near.wait_recv()
            block = self.at(near_row)
            self.copies += [push(block, block, row_peer(2 * d)) for d in (1, 2, 3)]

        def finish(self):
            wait_all(self.copies)

    class RingGather:
        def __init__(self, row, whole, half):
            self.row, self.whole, self.half = row, whole, half

        def start(self):
            block = self.whole(self.row)
            self.ahead = push(block, block, row_peer(2))
            self.behind = push(block, block, row_peer(6))

        def relay(self):
            self.ahead.wait_recv()
            block = self.half((self.row + 6) % 8, 0)
            self.rest = [push(block, block, row_peer(2))]
            self.behind.wait_recv()
            block = self.half((self.row + 2) % 8, 1)
            self.rest.append(push(block, block, row_peer(6)))

        def finish(self):
            wait_all(self.rest)

    class ColGather:
        def __init__(self, at, rest, band):
            self.at, self.rest, self.band = at, rest, band
            self.y, self.core = [], []

        def start(self):
            self.z = [push(self.at(0), self.at(4 - d), z_peer(d)) for d in (1, 2, 3)]

        def own_y(self):
            block = self.at(0)
            self.y.append([push(block, block, y_peer(d)) for d in (1, 2, 3)])

        def rest_y(self):
            wait_all(self.z)
            self.y.append([push(self.rest, self.rest, y_peer(d)) for d in (1, 2, 3)])

        def to_core(self, d):
            if d:
                for copies in self.y:
                    copies[d - 1].wait_recv()
            block = self.band((y + 4 - d) % 4)
            self.core.append(push(block, block, core_peer))

        def finish(self):
            wait_all(self.core)

    gather_w = ColGather(
        lambda e: wbuf.at[e, rows(HW * (2 * y + core), HW), :],
        wbuf.at[1:4, rows(HW * (2 * y + core), HW), :],
        lambda other: wbuf.at[:, rows(HW * (2 * other + core), HW), :])
    gather_a = RowGather(lambda row: abuf.at[acore, lanes(LA * row, LA)])
    b_parts = (lambda row: bbuf.at[row, 0:FP, :]), (lambda row, i: bbuf.at[row, 112 * i:112 * i + 112, :])
    gather_b = RingGather(r, *b_parts)
    gather_bn = RingGather(near_row, *b_parts)
    b_near = push(bbuf.at[r, 0:FP, :], bbuf.at[r, 0:FP, :], (near_row, c))
    gather_b.start()


    base = used[0]
    used[0] += 4
    for d in range(4):
        copy = pltpu.make_async_remote_copy(
            src_ref=act, dst_ref=axb.at[zlo, x], send_sem=ssem.at[base + d], recv_sem=rsem.at[base + x],
            device_id=swap_target((zhi + d) % 4), device_id_type=MESH,
        )
        if d:
            copy.start()
            sent.append((copy, None))
        else:
            pl.when(jnp.logical_not(stays))(copy.start)
            sent.append((copy, jnp.logical_not(stays)))

    @pl.when(stays)
    def _():
        axb[zlo, x] = act[...]

    def act_wait():
        for s in range(4):
            copy = pltpu.make_async_remote_copy(
                src_ref=act, dst_ref=axb.at[zlo, x], send_sem=ssem.at[base], recv_sem=rsem.at[base + s],
                device_id=core_peer, device_id_type=MESH,
            )
            pl.when(jnp.logical_not(jnp.logical_and(stays, x == s)))(copy.wait_recv)

    a_block = abuf.at[arow, lanes(LA * r, LA)]
    a_pair = push(a_block, a_block, pair_peer)
    gather_w.own_y()
    gather_b.relay()
    gather_w.start()
    a_pair.wait_recv()
    gather_a.start_near()
    gather_a.start()
    b_near.wait_recv()
    gather_bn.start()
    dt[...] = jnp.zeros_like(dt)
    bt[...] = jnp.zeros_like(bt)
    act_wait()
    act_y = push(axb.at[yh], axb.at[yh], y_peer(2))
    gather_w.rest_y()
    gather_a.forward()
    gather_bn.relay()
    gather_a.finish()
    a_core = push(abuf.at[acore, :], abuf.at[acore, :], core_peer)

    a_core.wait_recv()
    act_y.wait_recv()
    total = nn(abuf[:, 0:320], axb[0, 0])
    for v in range(1, 8):
        total = total + nn(abuf[:, LA * v:LA * v + 320], axb[v % 2, v // 2])
    prow = rows(HP * kt, HP)
    pbuf[prow, lanes(1024 * yh, 256)] = jnp.concatenate(
        [total[0:64], total[128:192], total[64:128], total[192:256]], axis=0).T.astype(BF16)
    gather_p = ColGather(
        lambda e: pbuf.at[prow, lanes(1024 * yh + 256 * e, 256)],
        pbuf.at[prow, lanes(1024 * yh + 256, 768)],
        lambda other: pbuf.at[rows(HP * (2 * core + other % 2), HP), lanes(1024 * (other // 2), 1024)])
    gather_p.start()
    gather_p.own_y()
    for d in range(4):
        gather_w.to_core(d)
    gather_p.rest_y()
    gather_p.to_core(0)

    def chain_term(row):
        return nn(bbuf[row, 0:FP, 0:HB], wbuf[(row // 2 + 4 - zhi) % 4, rows(HB * (row % 2), HB), :])

    def panel(row):
        return lanes(1024 * (row % 2) + 256 * ((row // 2 + 4 - zhi) % 4), 256)

    own = panel(r)
    gather_w.finish()
    total = chain_term(r) + chain_term(near_row)
    gather_b.finish()
    gather_bn.finish()
    for d in (1, 2, 3):
        total = total + chain_term((r + 2 * d) % 8) + chain_term((near_row + 2 * d) % 8)
    ct[:, own] = total.astype(BF16)
    gather_c = RowGather(lambda row: ct.at[:, panel(row)])
    c_ag = [push(ct.at[:, own], ct.at[:, own], row_peer(d)) for d in range(1, 8)]

    for v in range(8):
        bbuft[v] = bbuf[v].T
    for d in (1, 2, 3):
        gather_p.to_core(d)
    gather_p.finish()
    loads[4].wait()
    wait_all(c_ag)

    for k in range(4):
        t = KT[k]
        hidden = nt(ct[...], pbuf[HP * t:HP * t + HP, :])[0:216, :]
        s = 1.0 / (1.0 + jnp.exp(-hidden))
        grad = cot[:, HP * k:HP * k + HP].astype(F32) * s * (1.0 + hidden * (1.0 - s))
        dt[0:216, HP * t:HP * t + HP] = grad.astype(BF16)

    delta[...] = dt[...].T

    def tiles(body):
        lax.fori_loop(0, 8, lambda i, _: (body(lanes(256 * i, 256)), 0)[1], 0)

    def q_far(at):
        qfar[:, at] = nn(delta[rows(2 * HP * far, 2 * HP), 0:FP], ct[:, at]).astype(BF16)

    def q_sum(at):
        value = nn(delta[rows(2 * HP * core, 2 * HP), 0:FP], ct[:, at]) + qgot[:, at].astype(F32)
        qown[:, at] = value
        qhalf[:, at] = value.astype(BF16)

    tiles(q_far)
    q_core = push(qfar, qgot, core_peer)

    b_rs = []
    for d in range(1, 8):
        bs[d - 1] = nn(dt[0:FP, :], pbuf[:, panel((r + d) % 8)]).astype(BF16)
        b_rs.append(push(bs.at[d - 1], brcv.at[d - 1], row_peer(d)))
    back = nn(dt[0:FP, :], pbuf[:, own])

    q_core.wait_recv()
    tiles(q_sum)
    q_y = [
        [push(qhalf.at[rows(HP * ((y + d) % 2) + off, size), lanes(1024 * (((y + d) % 4) // 2), 1024)],
              qry.at[d - 1, off:off + size, :], y_peer(d)) for d in (1, 2, 3)]
        for off, size in CQ
    ]

    for d in range(7):
        b_rs[d].wait_recv()
        back = back + brcv[d].astype(F32)
    bt[0:FP, :] = (back * scale).astype(BF16)

    def cols_term(row):
        return nt(bt[0:FP, :], wbuf[(row // 2 + 4 - zhi) % 4, rows(HB * (row % 2), HB), :])

    class RingSum:
        def __init__(self, i, row):
            self.i, self.row = i, row

        def start(self):
            self.relayed = []
            for d, slot in ((2, 0), (1, 1), (3, 2)):
                gcs[self.i, slot, :, 0:HB] = cols_term((self.row + 2 * d) % 8).astype(BF16)
                if d == 2:
                    for h, peer in ((0, 2), (1, 6)):
                        self.relayed.append(push(
                            gcs.at[self.i, 0, 112 * h:112 * h + 112, :], gcr.at[self.i, h], row_peer(peer)))
            self.direct = []
            for slot, h, peer in ((1, 1, 2), (2, 0, 6)):
                block = slice(112 * h, 112 * h + 112)
                self.direct.append(push(
                    gcs.at[self.i, slot, block, :], gcx.at[self.i, slot - 1, block, :], row_peer(peer)))

        def relay(self):
            for slot, h, peer in ((1, 0, 2), (2, 1, 6)):
                block = slice(112 * h, 112 * h + 112)
                self.relayed[h].wait_recv()
                value = gcs[self.i, slot, block, 0:HB].astype(F32) + gcr[self.i, h, :, 0:HB].astype(F32)
                gcs[self.i, slot, block, 0:HB] = value.astype(BF16)
                self.direct.append(push(
                    gcs.at[self.i, slot, block, :], gcx.at[self.i, slot - 1, block, :], row_peer(peer)))

        def result(self, value):
            wait_all(self.direct)
            return value + gcx[self.i, 0, :, 0:HB].astype(F32) + gcx[self.i, 1, :, 0:HB].astype(F32)

    cols_near, cols_own = RingSum(0, near_row), RingSum(1, r)
    cols_near.start()

    def small_term(v, u, which):
        return nn(bbuft[v, rows(HW * (2 * u + which), HW), :], bt[...])

    for v in range(8):
        for u in range(2):
            gfar[v // 2, 2 * (v % 2) + u] = small_term(v, u, far).astype(BF16)
    g_core = push(gfar, ggot, core_peer)

    q_z = []
    for i, (off, size) in enumerate(CQ):
        wait_all(q_y[i])
        part = slice(off, off + size)
        for v in range(4):
            at = slice(256 * v, 256 * v + 256)
            value = qown[rows(HP * yl + off, size), lanes(1024 * yh + 256 * v, 256)]
            for d in range(3):
                value = value + qry[d, part, at].astype(F32)
            qyf[part, at] = value
            qys[part, at] = value.astype(BF16)
        q_z.append([
            push(qys.at[part, 256 * d:256 * d + 256], qrz.at[d - 1, part, :], z_peer(d))
            for d in (1, 2, 3)
        ])

    cols_own.start()
    g_core.wait_recv()
    for v in range(8):
        for u in range(2):
            at = v // 2, 2 * (v % 2) + u
            value = small_term(v, u, core) + ggot[at].astype(F32)
            gown[at] = value
            ghalf[at] = value.astype(BF16)

    def small_y(i):
        off, size = CW[i]
        return [
            push(ghalf.at[:, (y + d) % 4, off:off + size, :], gry.at[d - 1, :, off:off + size, :], y_peer(d))
            for d in (1, 2, 3)
        ]

    g_y = [small_y(0), small_y(1)]
    cols_near.relay()

    for copies in q_z:
        wait_all(copies)
    value = qyf[:, 0:256]
    for d in range(3):
        value = value + qrz[d].astype(F32)
    qt[...] = (value * scale).T.astype(BF16)
    for v in range(8):
        hfull[v, :, 0:320] = nt(qt[...], axb[v % 2, v // 2])
    for u in range(2):
        hs[:, 64 * u:64 * u + 64, 0:320] = hfull[:, rows(64 * (2 * u + far), 64), 0:320].astype(BF16)
    h_core = push(hs, hc, core_peer)
    h_core.wait_recv()
    for v in range(8):
        for u in range(2):
            value = hfull[v, rows(64 * (2 * u + core), 64), 0:320] + hc[v, 64 * u:64 * u + 64, 0:320].astype(F32)
            hyf[v, u, :, 0:320] = value
            hh[v, u, :, 0:320] = value.astype(BF16)
    h_r = [push(hh.at[(r + d) % 8], hr.at[d - 1], row_peer(d)) for d in range(1, 8)]

    cols_own.relay()
    gcn[...] = cols_term(near_row)
    gcf[...] = cols_term(r)

    def small_z(i):
        off, size = CW[i]
        wait_all(g_y[i])
        for v in range(4):
            value = gown[v, y, off:off + size, :]
            for d in range(3):
                value = value + gry[d, v, off:off + size, :].astype(F32)
            gyf[v, off:off + size, :] = value
            gys[v, off:off + size, :] = value.astype(BF16)
        return [
            push(gys.at[(zhi + d) % 4, off:off + size, :], grz.at[d - 1, off:off + size, :], z_peer(d))
            for d in (1, 2, 3)
        ]

    g_z = [small_z(0)]

    gce[:, 0:HB] = cols_near.result(gcn[...]).astype(BF16)
    gc_z = push(gce, gcz, (near_row, c))

    wait_all(h_r)
    for u in range(2):
        value = hyf[r, u, :, 0:320]
        for d in range(7):
            value = value + hr[d, u, :, 0:320].astype(F32)
        hp[u, :, 0:320] = value
        hq[u, :, 0:320] = value.astype(BF16)
    h_pair = push(hq.at[1 - yl], hy, pair_peer)
    g_z.append(small_z(1))

    value = cols_own.result(gcf[...])
    gc_z.wait_recv()
    value = (value + gcz[:, 0:HB].astype(F32)).astype(BF16)
    for k in range(4):
        gc[:, 172 * k:172 * k + 172] = value[0:216, HW * k:HW * k + 172]
    gc_copy = pltpu.make_async_copy(gc, gc_out, lsem.at[5])
    gc_copy.start()

    h_pair.wait_recv()
    gr_out[...] = (hp[yl, :, 0:320] + hy[:, 0:320].astype(F32)).astype(BF16)

    for copies in g_z:
        wait_all(copies)
    value = gyf[zhi]
    for d in range(3):
        value = value + grz[d].astype(F32)
    gs_out[...] = value[0:172, :].astype(BF16)

    gc_copy.wait()
    for copy, cond in sent:
        if cond is None:
            copy.wait_send()
        else:
            pl.when(cond)(copy.wait_send)


def store(gr, gc, gs, gr_out, gc_out, gs_out):
    gr_out[...] = gr[...]
    gc_out[...] = gc[...]
    gs_out[...] = gs[...]


def local(activations, cotangent, small_weight, grow_rows, grow_cols):
    scale = float(32 * activations.shape[0]) ** -0.5
    bf, f32 = (lambda *s: pltpu.VMEM(s, BF16)), (lambda *s: pltpu.VMEM(s, F32))
    scratch = [
        bf(320, 128), bf(216, 512), bf(172, 256), bf(64, 320), bf(216, 688), bf(216, 688),
        bf(HW, 256), bf(4, 8 * HW, 256), bf(8, 256, LB), bf(8, LB, 256), bf(64, LA), bf(256, 8 * LA),
        bf(2, 4, 320, 128),
        bf(512, 2048), bf(FP, 2048), bf(512, 256), bf(256, 512),
        bf(7, FP, 256), bf(7, FP, 256), bf(256, 256),
        bf(2 * HP, 2048), bf(2 * HP, 2048), f32(2 * HP, 2048), bf(2 * HP, 2048),
        bf(3, HP, 1024), f32(HP, 1024), bf(HP, 1024), bf(3, HP, 256), bf(256, 128),
        bf(4, 4, HW, 256), bf(4, 4, HW, 256), f32(4, 4, HW, 256), bf(4, 4, HW, 256),
        bf(3, 4, HW, 256), f32(4, HW, 256), bf(4, HW, 256), bf(3, HW, 256),
        bf(2, 3, FP, LB), bf(2, 2, FP, LB), bf(2, 2, 112, LB), bf(FP, LB), f32(FP, HB), f32(FP, HB), bf(FP, LB),
        f32(8, 256, LA), bf(8, 128, LA), bf(8, 128, LA), bf(8, 2, 64, LA), f32(8, 2, 64, LA),
        bf(7, 2, 64, LA), f32(2, 64, LA), bf(2, 64, LA), bf(64, LA),
        pltpu.SemaphoreType.DMA((NSEM,)), pltpu.SemaphoreType.DMA((NSEM,)), pltpu.SemaphoreType.DMA((6,)),
    ]
    vmem, hbm = pl.BlockSpec(memory_space=pltpu.VMEM), pl.BlockSpec(memory_space=pl.ANY)
    out_shape = (
        jax.ShapeDtypeStruct((64, 320), BF16),
        jax.ShapeDtypeStruct((216, 688), BF16),
        jax.ShapeDtypeStruct((172, 256), BF16),
    )
    results = pl.pallas_call(
        functools.partial(kernel, scale),
        out_shape=out_shape,
        in_specs=[hbm] * 5,
        out_specs=(vmem, hbm, vmem),
        scratch_shapes=scratch,
        compiler_params=pltpu.CompilerParams(
            collective_id=0, has_side_effects=True, vmem_limit_bytes=60 * 2**20
        ),
        cost_estimate=pl.CostEstimate(flops=3_700_000_000, bytes_accessed=3_000_000, transcendentals=110_592),
        name="grow",
    )(activations.T, cotangent.T, small_weight.T, grow_rows.T, grow_cols)
    gr, gc, gs = pl.pallas_call(
        store,
        out_shape=out_shape,
        in_specs=[vmem] * 3,
        out_specs=(vmem,) * 3,
        name="store",
    )(*results)
    return gr.T, gc, gs.T


def solution(mesh):
    return jax.shard_map(
        local,
        mesh=mesh,
        in_specs=(
            P("col", "row"),
            P("row", "col"),
            P("row", "col"),
            P("row", "col"),
            P("col", "row"),
        ),
        out_specs=(P("row", "col"), P("col", "row"), P("row", "col")),
        check_vma=False,
    )
```

```python
import functools

import jax
import jax.numpy as jnp
from jax import lax
from jax.experimental import pallas as pl
from jax.experimental.pallas import tpu as pltpu
from jax.sharding import PartitionSpec as P

MESH = pl.DeviceIdType.MESH
F32 = jnp.float32
BF16 = jnp.bfloat16
HW = 176
HP = 128
FP = 224
HB = 4 * HW
LB = 768
LA = 384
NSEM = 256
KT = (0, 2, 1, 3)
CW = ((0, 96), (96, 80))
CQ = ((0, 32), (32, 32), (64, 32), (96, 32))


def nn(a, b):
    return jnp.dot(a, b, preferred_element_type=F32)


def nt(a, b):
    return lax.dot_general(a, b, (((1,), (1,)), ((), ())), preferred_element_type=F32)


def lanes(start, size):
    return pl.ds(pl.multiple_of(start, 128), size)


def rows(start, size):
    return pl.ds(pl.multiple_of(start, 16), size)


def kernel(
    scale,
    act_in, cot_in, w_in, a_in, b_in,
    gr_out, gc_out, gs_out,
    act, cot, w, a, b, gc,
    wpad, wbuf, bbuf, bbuft, apad, abuf, axb,
    pbuf, ct, delta, dt,
    bs, brcv, bt,
    qfar, qgot, qown, qhalf, qry, qyf, qys, qrz, qt,
    gfar, ggot, gown, ghalf, gry, gyf, gys, grz,
    gcs, gcx, gcr, gce, gcf, gcn, gcz,
    hfull, hs, hc, hh, hyf, hr, hp, hq, hy,
    ssem, rsem, lsem,
):
    r = lax.axis_index("row")
    c = lax.axis_index("col")
    x, zlo = r // 2, r % 2
    zhi, y, core = c // 8, (c // 2) % 4, c % 2
    yh, yl = y // 2, y % 2
    kt = 2 * core + yl
    kn = 2 * yl + core
    far = 1 - core
    near_row = r + 1 - 2 * zlo
    stays = jnp.logical_and(x == zhi, zlo == yh)

    def row_peer(d):
        return ((r + d) % 8, c)

    def y_peer(d):
        return (r, zhi * 8 + ((y + d) % 4) * 2 + core)

    def z_peer(d):
        return (r, ((zhi + d) % 4) * 8 + y * 2 + core)

    core_peer = (r, c + 1 - 2 * core)
    pair_peer = (r, zhi * 8 + (y + 1 - 2 * yl) * 2 + core)

    def swap_target(j):
        return (zhi * 2 + yh, j * 8 + zlo * 4 + yl * 2 + core)

    def swap_source(s):
        return (s * 2 + yh, x * 8 + zlo * 4 + yl * 2 + core)

    used = [0]
    sent = []

    def push(src, dst, device):
        i = used[0]
        used[0] += 1
        copy = pltpu.make_async_remote_copy(
            src_ref=src, dst_ref=dst, send_sem=ssem.at[i], recv_sem=rsem.at[i],
            device_id=device, device_id_type=MESH,
        )
        copy.start()
        sent.append((copy, None))
        return copy

    def wait_all(copies):
        for copy in copies:
            copy.wait_recv()

    barrier = pltpu.get_barrier_semaphore()

    def greet(device):
        pl.semaphore_signal(barrier, inc=1, device_id=device, device_id_type=MESH)

    for d in range(1, 8):
        greet(row_peer(d))
    for d in range(1, 4):
        greet(y_peer(d))
        greet(z_peer(d))
    greet(core_peer)
    for s in range(4):
        pl.when(jnp.logical_not(jnp.logical_and(stays, x == s)))(lambda s=s: greet(swap_source(s)))

    loads = [
        pltpu.make_async_copy(src, dst, lsem.at[i])
        for i, (src, dst) in enumerate(((act_in, act), (w_in, w), (a_in, a), (b_in, b), (cot_in, cot)))
    ]
    for load in loads:
        load.start()
    bbuf[:, FP:256, :] = jnp.zeros((8, 256 - FP, LB), BF16)
    bbuf[r] = jnp.zeros((256, LB), BF16)
    loads[1].wait()
    wpad[0:172, :] = w[...]
    wpad[172:HW, :] = jnp.zeros((HW - 172, 256), BF16)
    wbuf[0, rows(HW * (2 * y + core), HW), :] = wpad[...]
    loads[2].wait()
    apad[:, 0:320] = a[...]
    apad[:, 320:LA] = jnp.zeros((64, LA - 320), BF16)
    arow = rows(64 * kt, 64)
    acore = rows(128 * core, 128)
    abuf[arow, lanes(LA * r, LA)] = apad[...]

    loads[3].wait()
    for k in range(4):
        bbuf[r, 0:216, HW * k:HW * k + 172] = b[:, 172 * k:172 * k + 172]
    loads[0].wait()

    @pl.when(stays)
    def _():
        pl.semaphore_wait(barrier, 17)

    @pl.when(jnp.logical_not(stays))
    def _():
        pl.semaphore_wait(barrier, 18)

    class RowGather:
        def __init__(self, at):
            self.at = at

        def start(self):
            block = self.at(r)
            self.copies = [push(block, block, row_peer(2 * d)) for d in (1, 2, 3)]

        def start_near(self):
            block = self.at(r)
            self.near = push(block, block, (near_row, c))

        def forward(self):
            self.near.wait_recv()
            block = self.at(near_row)
            self.copies += [push(block, block, row_peer(2 * d)) for d in (1, 2, 3)]

        def finish(self):
            wait_all(self.copies)

    class RingGather:
        def __init__(self, row, whole, half):
            self.row, self.whole, self.half = row, whole, half

        def start(self):
            block = self.whole(self.row)
            self.ahead = push(block, block, row_peer(2))
            self.behind = push(block, block, row_peer(6))

        def relay(self):
            self.ahead.wait_recv()
            block = self.half((self.row + 6) % 8, 0)
            self.rest = [push(block, block, row_peer(2))]
            self.behind.wait_recv()
            block = self.half((self.row + 2) % 8, 1)
            self.rest.append(push(block, block, row_peer(6)))

        def finish(self):
            wait_all(self.rest)

    class ColGather:
        def __init__(self, at, rest, band):
            self.at, self.rest, self.band = at, rest, band
            self.y, self.core = [], []

        def start(self):
            self.z = [push(self.at(0), self.at(4 - d), z_peer(d)) for d in (1, 2, 3)]

        def own_y(self):
            block = self.at(0)
            self.y.append([push(block, block, y_peer(d)) for d in (1, 2, 3)])

        def rest_y(self):
            wait_all(self.z)
            self.y.append([push(self.rest, self.rest, y_peer(d)) for d in (1, 2, 3)])

        def to_core(self, d):
            if d:
                for copies in self.y:
                    copies[d - 1].wait_recv()
            block = self.band((y + 4 - d) % 4)
            self.core.append(push(block, block, core_peer))

        def finish(self):
            wait_all(self.core)

    gather_w = ColGather(
        lambda e: wbuf.at[e, rows(HW * (2 * y + core), HW), :],
        wbuf.at[1:4, rows(HW * (2 * y + core), HW), :],
        lambda other: wbuf.at[:, rows(HW * (2 * other + core), HW), :])
    gather_a = RowGather(lambda row: abuf.at[acore, lanes(LA * row, LA)])
    b_parts = (lambda row: bbuf.at[row, 0:FP, :]), (lambda row, i: bbuf.at[row, 112 * i:112 * i + 112, :])
    gather_b = RingGather(r, *b_parts)
    gather_bn = RingGather(near_row, *b_parts)
    b_near = push(bbuf.at[r, 0:FP, :], bbuf.at[r, 0:FP, :], (near_row, c))
    gather_b.start()


    base = used[0]
    used[0] += 4
    for d in range(4):
        copy = pltpu.make_async_remote_copy(
            src_ref=act, dst_ref=axb.at[zlo, x], send_sem=ssem.at[base + d], recv_sem=rsem.at[base + x],
            device_id=swap_target((zhi + d) % 4), device_id_type=MESH,
        )
        if d:
            copy.start()
            sent.append((copy, None))
        else:
            pl.when(jnp.logical_not(stays))(copy.start)
            sent.append((copy, jnp.logical_not(stays)))

    @pl.when(stays)
    def _():
        axb[zlo, x] = act[...]

    def act_wait():
        for s in range(4):
            copy = pltpu.make_async_remote_copy(
                src_ref=act, dst_ref=axb.at[zlo, x], send_sem=ssem.at[base], recv_sem=rsem.at[base + s],
                device_id=core_peer, device_id_type=MESH,
            )
            pl.when(jnp.logical_not(jnp.logical_and(stays, x == s)))(copy.wait_recv)

    a_block = abuf.at[arow, lanes(LA * r, LA)]
    a_pair = push(a_block, a_block, pair_peer)
    gather_w.own_y()
    gather_b.relay()
    gather_w.start()
    a_pair.wait_recv()
    gather_a.start_near()
    gather_a.start()
    b_near.wait_recv()
    gather_bn.start()
    dt[...] = jnp.zeros_like(dt)
    bt[...] = jnp.zeros_like(bt)
    act_wait()
    act_y = push(axb.at[yh], axb.at[yh], y_peer(2))
    gather_w.rest_y()
    gather_a.forward()
    gather_bn.relay()
    gather_a.finish()
    a_core = push(abuf.at[acore, :], abuf.at[acore, :], core_peer)

    a_core.wait_recv()
    act_y.wait_recv()
    total = nn(abuf[:, 0:320], axb[0, 0])
    for v in range(1, 8):
        total = total + nn(abuf[:, LA * v:LA * v + 320], axb[v % 2, v // 2])
    prow = rows(HP * kt, HP)
    pbuf[prow, lanes(1024 * yh, 256)] = jnp.concatenate(
        [total[0:64], total[128:192], total[64:128], total[192:256]], axis=0).T.astype(BF16)
    gather_p = ColGather(
        lambda e: pbuf.at[prow, lanes(1024 * yh + 256 * e, 256)],
        pbuf.at[prow, lanes(1024 * yh + 256, 768)],
        lambda other: pbuf.at[rows(HP * (2 * core + other % 2), HP), lanes(1024 * (other // 2), 1024)])
    gather_p.start()
    gather_p.own_y()
    for d in range(4):
        gather_w.to_core(d)
    gather_p.rest_y()
    gather_p.to_core(0)

    def chain_term(row):
        return nn(bbuf[row, 0:FP, 0:HB], wbuf[(row // 2 + 4 - zhi) % 4, rows(HB * (row % 2), HB), :])

    def panel(row):
        return lanes(1024 * (row % 2) + 256 * ((row // 2 + 4 - zhi) % 4), 256)

    own = panel(r)
    gather_w.finish()
    total = chain_term(r) + chain_term(near_row)
    gather_b.finish()
    gather_bn.finish()
    for d in (1, 2, 3):
        total = total + chain_term((r + 2 * d) % 8) + chain_term((near_row + 2 * d) % 8)
    ct[:, own] = total.astype(BF16)
    gather_c = RowGather(lambda row: ct.at[:, panel(row)])
    c_ag = [push(ct.at[:, own], ct.at[:, own], row_peer(d)) for d in range(1, 8)]

    for v in range(8):
        bbuft[v] = bbuf[v].T
    for d in (1, 2, 3):
        gather_p.to_core(d)
    gather_p.finish()
    loads[4].wait()
    wait_all(c_ag)

    for k in range(4):
        t = KT[k]
        hidden = nt(ct[...], pbuf[HP * t:HP * t + HP, :])[0:216, :]
        s = 1.0 / (1.0 + jnp.exp(-hidden))
        grad = cot[:, HP * k:HP * k + HP].astype(F32) * s * (1.0 + hidden * (1.0 - s))
        dt[0:216, HP * t:HP * t + HP] = grad.astype(BF16)

    delta[...] = dt[...].T

    def tiles(body):
        lax.fori_loop(0, 8, lambda i, _: (body(lanes(256 * i, 256)), 0)[1], 0)

    def q_far(at):
        qfar[:, at] = nn(delta[rows(2 * HP * far, 2 * HP), 0:FP], ct[:, at]).astype(BF16)

    def q_sum(at):
        value = nn(delta[rows(2 * HP * core, 2 * HP), 0:FP], ct[:, at]) + qgot[:, at].astype(F32)
        qown[:, at] = value
        qhalf[:, at] = value.astype(BF16)

    tiles(q_far)
    q_core = push(qfar, qgot, core_peer)

    b_rs = []
    for d in range(1, 8):
        bs[d - 1] = nn(dt[0:FP, :], pbuf[:, panel((r + d) % 8)]).astype(BF16)
        b_rs.append(push(bs.at[d - 1], brcv.at[d - 1], row_peer(d)))
    back = nn(dt[0:FP, :], pbuf[:, own])

    q_core.wait_recv()
    tiles(q_sum)
    q_y = [
        [push(qhalf.at[rows(HP * ((y + d) % 2) + off, size), lanes(1024 * (((y + d) % 4) // 2), 1024)],
              qry.at[d - 1, off:off + size, :], y_peer(d)) for d in (1, 2, 3)]
        for off, size in CQ
    ]

    for d in range(7):
        b_rs[d].wait_recv()
        back = back + brcv[d].astype(F32)
    bt[0:FP, :] = (back * scale).astype(BF16)

    def cols_term(row):
        return nt(bt[0:FP, :], wbuf[(row // 2 + 4 - zhi) % 4, rows(HB * (row % 2), HB), :])

    class RingSum:
        def __init__(self, i, row):
            self.i, self.row = i, row

        def start(self):
            self.relayed = []
            for d, slot in ((2, 0), (1, 1), (3, 2)):
                gcs[self.i, slot, :, 0:HB] = cols_term((self.row + 2 * d) % 8).astype(BF16)
                if d == 2:
                    for h, peer in ((0, 2), (1, 6)):
                        self.relayed.append(push(
                            gcs.at[self.i, 0, 112 * h:112 * h + 112, :], gcr.at[self.i, h], row_peer(peer)))
            self.direct = []
            for slot, h, peer in ((1, 1, 2), (2, 0, 6)):
                block = slice(112 * h, 112 * h + 112)
                self.direct.append(push(
                    gcs.at[self.i, slot, block, :], gcx.at[self.i, slot - 1, block, :], row_peer(peer)))

        def relay(self):
            for slot, h, peer in ((1, 0, 2), (2, 1, 6)):
                block = slice(112 * h, 112 * h + 112)
                self.relayed[h].wait_recv()
                value = gcs[self.i, slot, block, 0:HB].astype(F32) + gcr[self.i, h, :, 0:HB].astype(F32)
                gcs[self.i, slot, block, 0:HB] = value.astype(BF16)
                self.direct.append(push(
                    gcs.at[self.i, slot, block, :], gcx.at[self.i, slot - 1, block, :], row_peer(peer)))

        def result(self, value):
            wait_all(self.direct)
            return value + gcx[self.i, 0, :, 0:HB].astype(F32) + gcx[self.i, 1, :, 0:HB].astype(F32)

    cols_near, cols_own = RingSum(0, near_row), RingSum(1, r)
    cols_near.start()

    def small_term(v, u, which):
        return nn(bbuft[v, rows(HW * (2 * u + which), HW), :], bt[...])

    for v in range(8):
        for u in range(2):
            gfar[v // 2, 2 * (v % 2) + u] = small_term(v, u, far).astype(BF16)
    g_core = push(gfar, ggot, core_peer)

    q_z = []
    for i, (off, size) in enumerate(CQ):
        wait_all(q_y[i])
        part = slice(off, off + size)
        for v in range(4):
            at = slice(256 * v, 256 * v + 256)
            value = qown[rows(HP * yl + off, size), lanes(1024 * yh + 256 * v, 256)]
            for d in range(3):
                value = value + qry[d, part, at].astype(F32)
            qyf[part, at] = value
            qys[part, at] = value.astype(BF16)
        q_z.append([
            push(qys.at[part, 256 * d:256 * d + 256], qrz.at[d - 1, part, :], z_peer(d))
            for d in (1, 2, 3)
        ])

    cols_own.start()
    g_core.wait_recv()
    for v in range(8):
        for u in range(2):
            at = v // 2, 2 * (v % 2) + u
            value = small_term(v, u, core) + ggot[at].astype(F32)
            gown[at] = value
            ghalf[at] = value.astype(BF16)

    def small_y(i):
        off, size = CW[i]
        return [
            push(ghalf.at[:, (y + d) % 4, off:off + size, :], gry.at[d - 1, :, off:off + size, :], y_peer(d))
            for d in (1, 2, 3)
        ]

    g_y = [small_y(0), small_y(1)]
    cols_near.relay()

    for copies in q_z:
        wait_all(copies)
    value = qyf[:, 0:256]
    for d in range(3):
        value = value + qrz[d].astype(F32)
    qt[...] = (value * scale).T.astype(BF16)
    for v in range(8):
        hfull[v, :, 0:320] = nt(qt[...], axb[v % 2, v // 2])
    for u in range(2):
        hs[:, 64 * u:64 * u + 64, 0:320] = hfull[:, rows(64 * (2 * u + far), 64), 0:320].astype(BF16)
    h_core = push(hs, hc, core_peer)
    h_core.wait_recv()
    for v in range(8):
        for u in range(2):
            value = hfull[v, rows(64 * (2 * u + core), 64), 0:320] + hc[v, 64 * u:64 * u + 64, 0:320].astype(F32)
            hyf[v, u, :, 0:320] = value
            hh[v, u, :, 0:320] = value.astype(BF16)
    h_r = [push(hh.at[(r + d) % 8], hr.at[d - 1], row_peer(d)) for d in range(1, 8)]

    cols_own.relay()
    gcn[...] = cols_term(near_row)
    gcf[...] = cols_term(r)

    def small_z(i):
        off, size = CW[i]
        wait_all(g_y[i])
        for v in range(4):
            value = gown[v, y, off:off + size, :]
            for d in range(3):
                value = value + gry[d, v, off:off + size, :].astype(F32)
            gyf[v, off:off + size, :] = value
            gys[v, off:off + size, :] = value.astype(BF16)
        return [
            push(gys.at[(zhi + d) % 4, off:off + size, :], grz.at[d - 1, off:off + size, :], z_peer(d))
            for d in (1, 2, 3)
        ]

    g_z = [small_z(0)]

    gce[:, 0:HB] = cols_near.result(gcn[...]).astype(BF16)
    gc_z = push(gce, gcz, (near_row, c))

    wait_all(h_r)
    for u in range(2):
        value = hyf[r, u, :, 0:320]
        for d in range(7):
            value = value + hr[d, u, :, 0:320].astype(F32)
        hp[u, :, 0:320] = value
        hq[u, :, 0:320] = value.astype(BF16)
    h_pair = push(hq.at[1 - yl], hy, pair_peer)
    g_z.append(small_z(1))

    value = cols_own.result(gcf[...])
    gc_z.wait_recv()
    value = (value + gcz[:, 0:HB].astype(F32)).astype(BF16)
    for k in range(4):
        gc[:, 172 * k:172 * k + 172] = value[0:216, HW * k:HW * k + 172]
    gc_copy = pltpu.make_async_copy(gc, gc_out, lsem.at[5])
    gc_copy.start()

    h_pair.wait_recv()
    gr_out[...] = (hp[yl, :, 0:320] + hy[:, 0:320].astype(F32)).astype(BF16)

    for copies in g_z:
        wait_all(copies)
    value = gyf[zhi]
    for d in range(3):
        value = value + grz[d].astype(F32)
    gs_out[...] = value[0:172, :].astype(BF16)

    gc_copy.wait()
    for copy, cond in sent:
        if cond is None:
            copy.wait_send()
        else:
            pl.when(cond)(copy.wait_send)


def store(gr, gc, gs, gr_out, gc_out, gs_out):
    gr_out[...] = gr[...]
    gc_out[...] = gc[...]
    gs_out[...] = gs[...]


def local(activations, cotangent, small_weight, grow_rows, grow_cols):
    scale = float(32 * activations.shape[0]) ** -0.5
    bf, f32 = (lambda *s: pltpu.VMEM(s, BF16)), (lambda *s: pltpu.VMEM(s, F32))
    scratch = [
        bf(320, 128), bf(216, 512), bf(172, 256), bf(64, 320), bf(216, 688), bf(216, 688),
        bf(HW, 256), bf(4, 8 * HW, 256), bf(8, 256, LB), bf(8, LB, 256), bf(64, LA), bf(256, 8 * LA),
        bf(2, 4, 320, 128),
        bf(512, 2048), bf(FP, 2048), bf(512, 256), bf(256, 512),
        bf(7, FP, 256), bf(7, FP, 256), bf(256, 256),
        bf(2 * HP, 2048), bf(2 * HP, 2048), f32(2 * HP, 2048), bf(2 * HP, 2048),
        bf(3, HP, 1024), f32(HP, 1024), bf(HP, 1024), bf(3, HP, 256), bf(256, 128),
        bf(4, 4, HW, 256), bf(4, 4, HW, 256), f32(4, 4, HW, 256), bf(4, 4, HW, 256),
        bf(3, 4, HW, 256), f32(4, HW, 256), bf(4, HW, 256), bf(3, HW, 256),
        bf(2, 3, FP, LB), bf(2, 2, FP, LB), bf(2, 2, 112, LB), bf(FP, LB), f32(FP, HB), f32(FP, HB), bf(FP, LB),
        f32(8, 256, LA), bf(8, 128, LA), bf(8, 128, LA), bf(8, 2, 64, LA), f32(8, 2, 64, LA),
        bf(7, 2, 64, LA), f32(2, 64, LA), bf(2, 64, LA), bf(64, LA),
        pltpu.SemaphoreType.DMA((NSEM,)), pltpu.SemaphoreType.DMA((NSEM,)), pltpu.SemaphoreType.DMA((6,)),
    ]
    vmem, hbm = pl.BlockSpec(memory_space=pltpu.VMEM), pl.BlockSpec(memory_space=pl.ANY)
    out_shape = (
        jax.ShapeDtypeStruct((64, 320), BF16),
        jax.ShapeDtypeStruct((216, 688), BF16),
        jax.ShapeDtypeStruct((172, 256), BF16),
    )
    results = pl.pallas_call(
        functools.partial(kernel, scale),
        out_shape=out_shape,
        in_specs=[hbm] * 5,
        out_specs=(vmem, hbm, vmem),
        scratch_shapes=scratch,
        compiler_params=pltpu.CompilerParams(
            collective_id=0, has_side_effects=True, vmem_limit_bytes=60 * 2**20
        ),
        cost_estimate=pl.CostEstimate(flops=3_700_000_000, bytes_accessed=3_000_000, transcendentals=110_592),
        name="grow",
    )(activations.T, cotangent.T, small_weight.T, grow_rows.T, grow_cols)
    gr, gc, gs = pl.pallas_call(
        store,
        out_shape=out_shape,
        in_specs=[vmem] * 3,
        out_specs=(vmem,) * 3,
        name="store",
    )(*results)
    return gr.T, gc, gs.T


def solution(mesh):
    return jax.shard_map(
        local,
        mesh=mesh,
        in_specs=(
            P("col", "row"),
            P("row", "col"),
            P("row", "col"),
            P("row", "col"),
            P("col", "row"),
        ),
        out_specs=(P("row", "col"), P("col", "row"), P("row", "col")),
        check_vma=False,
    )
```
